256 devices in a mesh: tok: 2 (over x_hi), out: 16 (over x_lo, y, core), inp: 8 (over z).
Axes of the slice: x: 4 (x_hi: 2, x_lo: 2; x = x_hi * 2 + x_lo), y: 4, z: 8, core: 2. Of those that a mesh axis runs over, the one named last changes fastest.
Arguments:
- cand_grad: bfloat16 [256, 28672], P(None, ('tok', 'inp'))
- cand_act: bfloat16 [256, 8192], P(None, ('tok', 'out'))
- query_grad: bfloat16 [64, 28672], P(None, ('tok', 'inp'))
- query_act: bfloat16 [64, 8192], P(None, ('tok', 'out'))
- eig_out: bfloat16 [28672, 28672], P(('tok', 'inp'), 'out'), may hold values from -0.03125 to 0.03125
- eig_in: bfloat16 [8192, 8192], P(('tok', 'out'), 'inp'), may hold values from -0.0625 to 0.0625
- eigenvalues: bfloat16 [28672, 8192], P('out', 'inp'), as said below
- doc_lengths: int32 [16], replicated, may hold values from 1 to 64, 256 in all
- query_ids: int32 [64], replicated, may hold values from 0 to 3, never falling along the last dimension, each value on 1 to 32 neighbouring positions
Outputs:
- scores: float32 [16, 4], replicated
The draws below stay inside these ranges and needn't reach their ends.
Inputs may be any that keep to these rules, and one draw needn't show every extreme that they name: `doc_lengths`: the lengths of the 16 documents sum to 256; the longest has exactly 64 tokens. `query_ids`: never falling; every query has one or more tokens, the longest exactly 32. `eigenvalues`: Positive.
All inputs are finite; a program needn't handle non-finite values.
Results may differ from the reference program's by a relative error of at most 0.0064.
Values may be sent and summed in bfloat16 or wider, within the bound.
A program may use at most 64 MiB of HBM per device.

```python
import math
import jax
import jax.numpy as jnp
import numpy as np
from jax import lax

D = 8192
FF = 28672
Q = 4
S = 64
DOCS = 16
CAND = 256
MOST = 64
QMOST = 32


def normal_rows(entry_key, row_count, col_count, factor):
    return jax.random.truncated_normal(entry_key, -6.0, 6.0, (row_count, col_count), jnp.float32) * factor


def band_levels(level_key, length, band_count, spread):
    levels = jnp.exp(jax.random.uniform(level_key, (band_count,), jnp.float32, -spread, spread))
    which = jnp.arange(length, dtype=jnp.int32) * band_count // length
    return levels[which]


def draw_cand_grad(key, part):
    key = jax.random.fold_in(key, 3)
    result = normal_rows(key, CAND, FF, 0.3 * FF ** (-0.25))
    return result.astype(jnp.bfloat16)


def draw_cand_act(key, part):
    key = jax.random.fold_in(key, 5)
    result = normal_rows(key, CAND, D, 0.3 * D ** (-0.25))
    return result.astype(jnp.bfloat16)


def draw_query_grad(key, part):
    key = jax.random.fold_in(key, 7)
    result = normal_rows(key, S, FF, 0.3 * FF ** (-0.25))
    return result.astype(jnp.bfloat16)


def draw_query_act(key, part):
    key = jax.random.fold_in(key, 9)
    result = normal_rows(key, S, D, 0.3 * D ** (-0.25))
    return result.astype(jnp.bfloat16)


def draw_eigenvalues(key, part):
    key = jax.random.fold_in(key, 11)
    jitter_key, row_key, col_key = jax.random.split(key, 3)
    row_frac = jnp.arange(FF, dtype=jnp.float32)[:, None] / FF
    col_frac = jnp.arange(D, dtype=jnp.float32)[None, :] / D
    row_level = band_levels(row_key, FF, 32, 1.5)[:, None]
    col_level = band_levels(col_key, D, 16, 1.5)[None, :]
    jitter = jax.random.uniform(jitter_key, (FF, D), jnp.float32, -1.5, 0.0)
    exponent = 0.7 - row_frac - 0.7 * col_frac + jitter
    return (jnp.power(10.0, exponent) * row_level * col_level).astype(jnp.bfloat16)


def shard_levels(own_key, shape, pieces, smallest, largest):
    factor_of = 1.0
    for position, parts in pieces:
        draws = jax.random.uniform(jax.random.fold_in(jax.random.fold_in(own_key, 6), position), (parts,), jnp.float32, smallest / len(pieces), largest / len(pieces))
        factor_of = factor_of * jnp.repeat(jnp.exp(draws), shape[position] // parts).reshape((-1,) + (1,) * (len(shape) - 1 - position))
    return factor_of


def length_profile(number_of, total, bound, slope):
    loads = [(1 << 20) // math.isqrt(standing ** slope) + 1 for standing in range(2, number_of + 1)]
    rest, given = total - bound - (number_of - 1), [1] * (number_of - 1)
    while rest > 0:
        free = [i for i in range(number_of - 1) if given[i] < bound]
        pool, remaining = sum([loads[i] for i in free]), rest
        for i in free:
            more = min(bound - given[i], max(1, remaining * loads[i] // pool), rest)
            given[i] = given[i] + more
            rest = rest - more
    return np.array([bound] + given)


def ragged(key, amount, total, limit, skew):
    if amount == 2:
        one = jax.random.randint(key, (), max(1, total - limit), min(limit, total - 1) + 1)
        return jnp.stack([one, total - one])
    sizes = jnp.asarray(length_profile(amount, total, limit, skew), jnp.int32)
    couples = (amount - 1) // 2
    donor, taker = sizes[1:1 + 2 * couples:2], sizes[2:2 + 2 * couples:2]
    room = jnp.minimum(donor - 1, limit - taker)
    moved = jax.random.randint(jax.random.fold_in(key, 1), (couples,), 0, 1 << 20) % (room + 1)
    sizes = sizes.at[1:1 + 2 * couples:2].set(donor - moved).at[2:2 + 2 * couples:2].set(taker + moved)
    return sizes[jax.random.permutation(jax.random.fold_in(key, 2), amount)]


def normal_values(stream_key, dims, width, bound, pieces=(), held_as=jnp.bfloat16):
    values = jax.random.normal(stream_key, dims, jnp.float32) * width
    if len(pieces) > 0:
        values = shard_levels(stream_key, dims, pieces, -0.22, 0.18) * values
    return jnp.clip(values, min=-bound, max=bound).astype(held_as)


def setup_inputs(seed: int = 0) -> dict:
    streams_of = jax.random.split(jax.random.key(seed), 10)
    cand_grad = draw_cand_grad(jax.random.fold_in(streams_of[9], 71), 0)
    cand_act = draw_cand_act(jax.random.fold_in(streams_of[9], 71), 0)
    query_grad = draw_query_grad(jax.random.fold_in(streams_of[9], 71), 0)
    query_act = draw_query_act(jax.random.fold_in(streams_of[9], 71), 0)
    eig_out = normal_values(streams_of[4], (FF, FF), FF ** -0.5, 0.03125, ((0, 16), (1, 16)))
    eig_in = normal_values(streams_of[5], (D, D), D ** -0.5, 0.0625, ((0, 32), (1, 8)))
    eigenvalues = draw_eigenvalues(jax.random.fold_in(streams_of[9], 71), 0)
    doc_lengths = ragged(streams_of[7], DOCS, CAND, MOST, 2).astype(jnp.int32)
    query_ids = jnp.searchsorted(jnp.cumsum(ragged(streams_of[8], Q, S, QMOST, 1)), jnp.arange(S), side="right").astype(jnp.int32)
    return dict(cand_grad=cand_grad, cand_act=cand_act, query_grad=query_grad, query_act=query_act, eig_out=eig_out, eig_in=eig_in, eigenvalues=eigenvalues, doc_lengths=doc_lengths, query_ids=query_ids)


def reference(cand_grad, cand_act, query_grad, query_act, eig_out, eig_in, eigenvalues, doc_lengths, query_ids):
    cand_rows = cand_grad.shape[0]
    rotated_grads = jnp.dot(jnp.concatenate([cand_grad, query_grad], 0), eig_out, preferred_element_type=jnp.float32).astype(jnp.bfloat16)
    rotated_acts = jnp.dot(jnp.concatenate([cand_act, query_act], 0), eig_in, preferred_element_type=jnp.float32).astype(jnp.bfloat16)
    cand_rotg = rotated_grads[:cand_rows]
    query_rotg = rotated_grads[cand_rows:]
    cand_rota = rotated_acts[:cand_rows].astype(jnp.float32)
    query_rota = rotated_acts[cand_rows:]
    values = eigenvalues.astype(jnp.float32)
    damping = 0.1 * jnp.sum(values) / (FF * D)
    inverse = 1.0 / (values + damping)
    columns = []
    for query_index in range(Q):
        weight = (query_ids == query_index).astype(jnp.bfloat16)
        weighted = query_rotg * weight[:, None]
        outer_sum = lax.dot_general(weighted, query_rota, (((0,), (0,)), ((), ())), preferred_element_type=jnp.float32)
        precond = (inverse * outer_sum).astype(jnp.bfloat16)
        projected = jnp.dot(cand_rotg, precond, preferred_element_type=jnp.float32)
        columns.append(jnp.sum(projected * cand_rota, axis=1))
    token_scores = jnp.stack(columns, 1)
    starts = jnp.cumsum(doc_lengths, dtype=jnp.int32) - doc_lengths
    positions = jnp.arange(cand_rows, dtype=jnp.int32)
    member = ((positions[:, None] >= starts[None, :]) & (positions[:, None] < (starts + doc_lengths)[None, :])).astype(jnp.float32)
    return lax.dot_general(member, token_scores, (((0,), (0,)), ((), ())), precision=lax.Precision.HIGHEST, preferred_element_type=jnp.float32)
```

```python
import jax
import jax.numpy as jnp
from jax import lax
from jax.experimental import pallas as pl
from jax.experimental.pallas import tpu as pltpu
from jax.sharding import PartitionSpec as P

D = 8192
FF = 28672
Q = 4
MESH = pl.DeviceIdType.MESH
F32 = jnp.float32
BF16 = jnp.bfloat16
GROUPS = 7
SETS = ((0, 1024), (1024, 768))
HALF = ((0, 512), (512, 384))


def kernel(
    cg, ca, qg, qa, eo, ei, ev, dl, qi, out,
    xg, xa, eob, eib, evb, gpc, gpq, rsc, rsq, gsc, gsq, rxc, rxq, gfc, gfq,
    apc, apq, rac, raq, rdc, rdq, afc, afq, inv, mm, ea, eb, fa, fb,
    ld, evs, rs_s, rs_r, x_s, x_r, ag_s, ag_r, co_s, co_r, pr_s, pr_r, st_s, st_r,
):
    tok, o, z = lax.axis_index("tok"), lax.axis_index("out"), lax.axis_index("inp")
    x = tok * 2 + o // 8
    y = lax.rem(o // 2, 4)
    c = lax.rem(o, 2)

    def dev(dx, dy, dc, dz):
        nx = lax.rem(x + dx, 4)
        ny = lax.rem(y + dy, 4)
        nc = lax.rem(c + dc, 2)
        return (nx // 2, lax.rem(nx, 2) * 8 + ny * 2 + nc, lax.rem(z + dz, 8))

    def remote(src, dst, ss, rs, where):
        return pltpu.make_async_remote_copy(
            src_ref=src, dst_ref=dst, send_sem=ss, recv_sem=rs, device_id=where, device_id_type=MESH
        )

    def line_peer(r):
        return dev(0, 0, r // 8, lax.rem(r, 8))

    def plane_peer(r):
        return dev(r // 4, lax.rem(r, 4), 0, 0)

    def each(body):
        lax.fori_loop(1, 16, lambda r, carry: (body(r), carry)[1], 0)

    loads = [
        pltpu.make_async_copy(ca, xa.at[pl.ds(0, 256)], ld.at[0]),
        pltpu.make_async_copy(qa, xa.at[pl.ds(256, 64)], ld.at[1]),
        pltpu.make_async_copy(ei, eib, ld.at[2]),
        pltpu.make_async_copy(cg, xg.at[pl.ds(0, 256)], ld.at[3]),
        pltpu.make_async_copy(qg, xg.at[pl.ds(256, 64)], ld.at[4]),
    ]

    def eo_load(g):
        return pltpu.make_async_copy(eo.at[:, pl.ds(pl.multiple_of(g * 256, 256), 256)], eob.at[g], ld.at[5 + g])

    def ev_load(g):
        row = pl.multiple_of((2 * g + tok) * 128, 128)
        return pltpu.make_async_copy(ev.at[pl.ds(row, 128)], evb.at[g], evs.at[g])

    for load in loads:
        load.start()
    for g in range(GROUPS):
        eo_load(g).start()

    barrier = pltpu.get_barrier_semaphore()

    def greet(r):
        pl.semaphore_signal(barrier, inc=1, device_id=line_peer(r), device_id_type=MESH)
        pl.semaphore_signal(barrier, inc=1, device_id=plane_peer(r), device_id_type=MESH)

    each(greet)
    for g in range(GROUPS):
        ev_load(g).start()

    for load in loads[:3]:
        load.wait()
    apart = jnp.dot(xa[...], eib[...], preferred_element_type=F32)
    apc[...] = apart[:256].astype(BF16)
    apq[...] = apart[256:]

    pl.semaphore_wait(barrier, 30)

    other = pl.ds(pl.multiple_of((1 - c) * 512, 512), 512)
    mine = pl.ds(pl.multiple_of(c * 512, 512), 512)
    core1 = [
        remote(apc.at[:, other], rac, co_s.at[0], co_r.at[0], dev(0, 0, 1, 0)),
        remote(apq.at[:, other], raq, co_s.at[1], co_r.at[1], dev(0, 0, 1, 0)),
    ]
    for copy in core1:
        copy.start()

    for load in loads[3:]:
        load.wait()

    def rotate(g, carry):
        eo_load(g).wait()
        part = jnp.dot(xg[...], eob[g], preferred_element_type=F32)
        cols = pl.ds(pl.multiple_of(g * 256, 256), 256)
        gpc[:, cols] = part[:256].astype(BF16)
        gpq[:, cols] = part[256:]
        return carry

    part_refs = (gpq, gpc)
    ring_refs = (rsq, rsc)
    heights = (8, 32)

    def rows(kind, owner):
        h = heights[kind]
        return pl.ds(pl.multiple_of(lax.rem(owner + 16, 8) * h, h), h)

    def hop(d):
        return dev(0, 0, 0, 1 if d == 0 else 7)

    def sign(d):
        return 1 if d == 0 else -1

    def rs_first(kind, d, s, cs):
        cols = pl.ds(*SETS[cs])
        return remote(
            part_refs[kind].at[rows(kind, z + sign(d) * (5 - s)), cols],
            ring_refs[kind].at[d, s - 1, :, cols],
            rs_s.at[kind, d, s - 1, cs], rs_r.at[kind, d, s - 1, cs], hop(d),
        )

    def rs_next(kind, d, s, cs):
        cols = pl.ds(*SETS[cs])
        return remote(
            ring_refs[kind].at[d, s - 2, :, cols],
            ring_refs[kind].at[d, s - 1, :, cols],
            rs_s.at[kind, d, s - 1, cs], rs_r.at[kind, d, s - 1, cs], hop(d),
        )

    def rs_copy(kind, d, s, cs):
        first = 1 if cs == d else 2
        return rs_first(kind, d, s, cs) if s == first else rs_next(kind, d, s, cs)

    def rs_step(kind, s):
        for d in range(2):
            for cs in ((d, 1 - d) if s > 1 else (d,)):
                rs_copy(kind, d, s, cs).wait_recv()
                cols = pl.ds(*SETS[cs])
                ref = ring_refs[kind]
                own = part_refs[kind][rows(kind, z + sign(d) * (4 - s)), cols].astype(F32)
                ref[d, s - 1, :, cols] = (ref[d, s - 1, :, cols].astype(F32) + own).astype(ref.dtype)
                rs_copy(kind, d, s + 1, cs).start()

    lax.fori_loop(0, 4, rotate, 0)
    for kind in range(2):
        rs_copy(kind, 0, 1, 0).start()
        rs_copy(kind, 1, 2, 0).start()
    lax.fori_loop(4, 7, rotate, 0)
    for kind in range(2):
        rs_copy(kind, 1, 1, 1).start()
        rs_copy(kind, 0, 2, 1).start()

    for copy in core1:
        copy.wait()
    rac[...] = (rac[...].astype(F32) + apc[:, mine].astype(F32)).astype(BF16)
    raq[...] = raq[...] + apq[:, mine]
    chip = x * 4 + y

    def a_scatter(r):
        nx = lax.rem(x + r // 4, 4)
        ny = lax.rem(y + lax.rem(r, 4), 4)
        cols = pl.ds(pl.multiple_of(ny * 128, 128), 128)
        return (
            remote(rac.at[pl.ds(pl.multiple_of(nx * 64, 64), 64), cols], rdc.at[chip],
                   pr_s.at[0, r], pr_r.at[0, r], plane_peer(r)),
            remote(raq.at[pl.ds(pl.multiple_of(nx * 16, 16), 16), cols], rdq.at[chip],
                   pr_s.at[1, r], pr_r.at[1, r], plane_peer(r)),
        )

    def start_both(pair):
        pair[0].start()
        pair[1].start()

    def recv_both(pair):
        pair[0].wait_recv()
        pair[1].wait_recv()

    def send_both(pair):
        pair[0].wait_send()
        pair[1].wait_send()

    each(lambda r: start_both(a_scatter(r)))
    own_rows_c = pl.ds(pl.multiple_of(x * 64, 64), 64)
    own_rows_q = pl.ds(pl.multiple_of(x * 16, 16), 16)
    own_cols = pl.ds(pl.multiple_of(y * 128, 128), 128)
    rdc[chip] = rac[own_rows_c, own_cols]
    rdq[chip] = raq[own_rows_q, own_cols]

    for kind in range(2):
        rs_step(kind, 1)

    line = c * 8 + z
    total = jnp.zeros((8, 128), F32)
    for g in range(GROUPS):
        ev_load(g).wait()
        for cb in range(8):
            vals = evb[g, :, cb * 128:(cb + 1) * 128].astype(F32)
            total = total + jnp.sum(vals.reshape(16, 8, 128), axis=0)

    def all_to(buf, slot, kind, peer):
        def body(r):
            return remote(buf.at[slot], buf.at[slot], st_s.at[kind, r], st_r.at[kind, r], peer(r))
        return body

    e_line = all_to(ea, line, 0, line_peer)
    e_plane = all_to(eb, chip, 1, plane_peer)
    f_line = all_to(fa, line, 2, line_peer)
    f_plane = all_to(fb, chip, 3, plane_peer)

    ea[line] = total
    each(lambda r: e_line(r).start())

    for kind in range(2):
        rs_step(kind, 2)

    each(lambda r: e_line(r).wait_recv())
    eb[chip] = jnp.sum(ea[...], axis=0)
    each(lambda r: e_plane(r).start())

    each(lambda r: recv_both(a_scatter(r)))
    piece_cols = pl.ds(pl.multiple_of(c * 512 + y * 128, 128), 128)
    afc[own_rows_c, piece_cols] = jnp.sum(rdc[...].astype(F32), axis=0).astype(BF16)
    afq[own_rows_q, piece_cols] = jnp.sum(rdq[...], axis=0).astype(BF16)

    def a_gather(r):
        return (
            remote(afc.at[own_rows_c, piece_cols], afc.at[own_rows_c, piece_cols],
                   pr_s.at[2, r], pr_r.at[2, r], plane_peer(r)),
            remote(afq.at[own_rows_q, piece_cols], afq.at[own_rows_q, piece_cols],
                   pr_s.at[3, r], pr_r.at[3, r], plane_peer(r)),
        )

    each(lambda r: start_both(a_gather(r)))

    for kind in range(2):
        rs_step(kind, 3)

    each(lambda r: e_plane(r).wait_recv())
    eigen_sum = jnp.sum(jnp.sum(eb[...], axis=0))
    damping = 0.1 * eigen_sum / (FF * D)

    def invert(g, carry):
        inv[g] = 1.0 / (evb[g].astype(F32) + damping)
        return carry

    lax.fori_loop(0, GROUPS, invert, 0)

    sum_refs = (gsq, gsc)
    x_refs = (rxq, rxc)
    full_refs = (gfq, gfc)

    def x_copy(kind, cs):
        cols = pl.ds(*HALF[cs])
        return remote(sum_refs[kind].at[1 - tok, :, cols], x_refs[kind].at[:, cols],
                      x_s.at[kind, cs], x_r.at[kind, cs], dev(2, 0, 0, 0))

    for kind in range(2):
        for cs in range(2):
            rs_copy(kind, 0, 4, cs).wait_recv()
            rs_copy(kind, 1, 4, cs).wait_recv()
            lo, size = SETS[cs]
            for g in range(lo // 256, (lo + size) // 256):
                for t in range(2):
                    cols = pl.ds(g * 256 + t * 128, 128)
                    value = (
                        part_refs[kind][rows(kind, z), cols].astype(F32)
                        + ring_refs[kind][0, 3, :, cols].astype(F32)
                        + ring_refs[kind][1, 3, :, cols].astype(F32)
                    )
                    sum_refs[kind][t, :, g * 128:(g + 1) * 128] = value.astype(sum_refs[kind].dtype)
            x_copy(kind, cs).start()

    def ag_copy(kind, d, s, cs):
        cols = pl.ds(*HALF[cs])
        at = rows(kind, z - sign(d) * (s - 1))
        return remote(full_refs[kind].at[at, cols], full_refs[kind].at[at, cols],
                      ag_s.at[kind, d, s - 1, cs], ag_r.at[kind, d, s - 1, cs], hop(d))

    for kind in range(2):
        for cs in range(2):
            x_copy(kind, cs).wait_recv()
            cols = pl.ds(*HALF[cs])
            value = sum_refs[kind][tok, :, cols].astype(F32) + x_refs[kind][:, cols].astype(F32)
            full_refs[kind][rows(kind, z), cols] = value.astype(BF16).astype(full_refs[kind].dtype)
            for d in range(2):
                ag_copy(kind, d, 1, cs).start()

    each(lambda r: recv_both(a_gather(r)))
    core2 = [
        remote(afc.at[:, mine], afc.at[:, mine], co_s.at[2], co_r.at[2], dev(0, 0, 1, 0)),
        remote(afq.at[:, mine], afq.at[:, mine], co_s.at[3], co_r.at[3], dev(0, 0, 1, 0)),
    ]
    for copy in core2:
        copy.start()

    ids = jnp.zeros((1, 64), jnp.int32)
    lane = lax.broadcasted_iota(jnp.int32, (1, 64), 1)
    for s in range(64):
        ids = jnp.where(lane == s, qi[s], ids)
    doc = lax.broadcasted_iota(jnp.int32, (16, 256), 0)
    position = lax.broadcasted_iota(jnp.int32, (16, 256), 1)
    first = jnp.zeros((16, 256), jnp.int32)
    last = jnp.zeros((16, 256), jnp.int32)
    start = jnp.int32(0)
    for n in range(16):
        stop = start + dl[n]
        first = jnp.where(doc == n, start, first)
        last = jnp.where(doc == n, stop, last)
        start = stop
    member = ((position >= first) & (position < last)).astype(F32)

    def ag_step(kind, s):
        for d in range(2):
            for cs in ((d, 1 - d) if s < 4 else (d,)):
                ag_copy(kind, d, s, cs).wait_recv()
                if s < 3 or (s == 3 and cs == d):
                    ag_copy(kind, d, s + 1, cs).start()

    for s in (1, 2, 3):
        for kind in range(2):
            ag_step(kind, s)
    for copy in core2:
        copy.wait()
    ag_step(0, 4)

    def contract(g, carry):
        cols = pl.ds(pl.multiple_of(g * 128, 128), 128)
        turned = gfq[:, cols].T
        stacked = jnp.concatenate(
            [jnp.where(ids == q, turned, 0.0).astype(BF16) for q in range(Q)], axis=0
        )
        outer = jnp.dot(stacked, afq[...], preferred_element_type=F32)
        scale = inv[g]
        precond = jnp.concatenate(
            [(scale * outer[q * 128:(q + 1) * 128]).astype(BF16) for q in range(Q)], axis=0
        )
        mm[g] = lax.dot_general(
            afc[...], precond, (((1,), (1,)), ((), ())), preferred_element_type=F32
        )
        return carry

    lax.fori_loop(0, GROUPS, contract, 0)
    ag_step(1, 4)

    columns = []
    for q in range(Q):
        acc = jnp.zeros((256, 128), F32)
        for g in range(GROUPS):
            acc = acc + gfc[:, g * 128:(g + 1) * 128].astype(F32) * mm[g, :, q * 128:(q + 1) * 128]
        columns.append(acc)
    spread = jnp.dot(
        member, jnp.concatenate(columns, axis=1), precision=lax.Precision.HIGHEST, preferred_element_type=F32
    )
    lanes = lax.broadcasted_iota(jnp.int32, (16, 128), 1)
    scores = jnp.zeros((16, 128), F32)
    for q in range(Q):
        column = jnp.sum(spread[:, q * 128:(q + 1) * 128], axis=1, keepdims=True)
        scores = jnp.where(lanes == q, column, scores)

    fa[line] = scores
    each(lambda r: f_line(r).start())
    each(lambda r: f_line(r).wait_recv())
    fb[chip] = jnp.sum(fa[...], axis=0)
    each(lambda r: f_plane(r).start())
    each(lambda r: f_plane(r).wait_recv())
    out[...] = jnp.sum(fb[...], axis=0)[:, :Q]

    for kind in range(2):
        for cs in range(2):
            x_copy(kind, cs).wait_send()
        for d in range(2):
            for s in range(1, 5):
                for cs in range(2):
                    if s > 1 or cs == d:
                        rs_copy(kind, d, s, cs).wait_send()
                    if s < 4 or cs == d:
                        ag_copy(kind, d, s, cs).wait_send()

    def drain(r):
        send_both(a_scatter(r))
        send_both(a_gather(r))
        for body in (e_line, e_plane, f_line, f_plane):
            body(r).wait_send()

    each(drain)


def local(*args):
    dma = pltpu.SemaphoreType.DMA
    vm = pltpu.VMEM
    return pl.pallas_call(
        kernel,
        out_shape=jax.ShapeDtypeStruct((16, Q), F32),
        in_specs=[pl.BlockSpec(memory_space=pl.ANY)] * 7 + [pl.BlockSpec(memory_space=pltpu.SMEM)] * 2,
        out_specs=pl.BlockSpec(memory_space=pltpu.VMEM),
        scratch_shapes=[
            vm((320, 1792), BF16), vm((320, 256), BF16), vm((GROUPS, 1792, 256), BF16), vm((256, 1024), BF16),
            vm((GROUPS, 128, 1024), BF16),
            vm((256, 1792), BF16), vm((64, 1792), F32),
            vm((2, 4, 32, 1792), BF16), vm((2, 4, 8, 1792), F32),
            vm((2, 32, 896), BF16), vm((2, 8, 896), F32),
            vm((32, 896), BF16), vm((8, 896), F32),
            vm((256, 896), BF16), vm((64, 896), F32),
            vm((256, 1024), BF16), vm((64, 1024), F32),
            vm((256, 512), BF16), vm((64, 512), F32),
            vm((16, 64, 128), BF16), vm((16, 16, 128), F32),
            vm((256, 1024), BF16), vm((64, 1024), BF16),
            vm((GROUPS, 128, 1024), F32), vm((GROUPS, 256, 512), F32),
            vm((16, 8, 128), F32), vm((16, 8, 128), F32), vm((16, 16, 128), F32), vm((16, 16, 128), F32),
            dma((5 + GROUPS,)), dma((GROUPS,)),
            dma((2, 2, 4, 2)), dma((2, 2, 4, 2)),
            dma((2, 2)), dma((2, 2)),
            dma((2, 2, 4, 2)), dma((2, 2, 4, 2)),
            dma((4,)), dma((4,)),
            dma((4, 16)), dma((4, 16)),
            dma((4, 16)), dma((4, 16)),
        ],
        name="influence",
        compiler_params=pltpu.CompilerParams(
            collective_id=0, has_side_effects=True, vmem_limit_bytes=52 << 20
        ),
    )(*args)


def solution(mesh):
    in_specs = (
        P(None, ("tok", "inp")),
        P(None, ("tok", "out")),
        P(None, ("tok", "inp")),
        P(None, ("tok", "out")),
        P(("tok", "inp"), "out"),
        P(("tok", "out"), "inp"),
        P("out", "inp"),
        P(),
        P(),
    )
    return jax.shard_map(local, mesh=mesh, in_specs=in_specs, out_specs=P(), check_vma=False)
```

```python
import jax
import jax.numpy as jnp
from jax import lax
from jax.experimental import pallas as pl
from jax.experimental.pallas import tpu as pltpu
from jax.sharding import PartitionSpec as P

D = 8192
FF = 28672
Q = 4
MESH = pl.DeviceIdType.MESH
F32 = jnp.float32
BF16 = jnp.bfloat16
GROUPS = 7
SETS = ((0, 512), (512, 384))


def kernel(
    cg, ca, qg, qa, eo, ei, ev, dl, qi, out,
    xg, xa, eob, eib, evb, gpc, gpq, rsc, rsq, oxc, oxq, gfc, gfq,
    apc, apq, rac, raq, rdc, rdq, afc, afq, inv, mm, ea, eb, fa, fb,
    ld, evs, rs_s, rs_r, ag_s, ag_r, co_s, co_r, pr_s, pr_r, st_s, st_r,
):
    tok, o, z = lax.axis_index("tok"), lax.axis_index("out"), lax.axis_index("inp")
    x = tok * 2 + o // 8
    y = lax.rem(o // 2, 4)
    c = lax.rem(o, 2)
    chip = x * 4 + y
    line = c * 8 + z

    def dev(dx, dy, dc, dz):
        nx = lax.rem(x + dx, 4)
        ny = lax.rem(y + dy, 4)
        nc = lax.rem(c + dc, 2)
        return (nx // 2, lax.rem(nx, 2) * 8 + ny * 2 + nc, lax.rem(z + dz, 8))

    def remote(src, dst, ss, rs, where):
        return pltpu.make_async_remote_copy(
            src_ref=src, dst_ref=dst, send_sem=ss, recv_sem=rs, device_id=where, device_id_type=MESH
        )

    def line_peer(r):
        n = r - 1 + r // 15
        j = n // 2
        odd = lax.rem(j, 2)
        dz = 4 + odd * ((j + 1) // 2) + (1 - odd) * (8 - j // 2)
        return dev(0, 0, lax.rem(n, 2), dz)

    def plane_shift(r):
        n = r - 1 + r // 11
        return lax.rem(2 + n // 4, 4), lax.rem(2 + lax.rem(n, 4), 4)

    def plane_peer(r):
        dx, dy = plane_shift(r)
        return dev(dx, dy, 0, 0)

    def each(body):
        lax.fori_loop(1, 16, lambda r, carry: (body(r), carry)[1], 0)

    sends, waits = [], {}

    def single(copy):
        return lambda do: do(copy)

    def several(copies):
        def run(do):
            for copy in copies:
                do(copy)
        return run

    def bundle(copies):
        def run(do):
            def body(r):
                for copy in copies(r):
                    do(copy)
            each(body)
        return run

    def send(key, run):
        run(lambda copy: copy.start())
        sends.append(run)
        waits[key] = run

    def arrive(key):
        waits.pop(key)(lambda copy: copy.wait_recv())

    def drain():
        while sends:
            sends.pop()(lambda copy: copy.wait_send())

    def finish():
        for key in list(waits):
            arrive(key)
        drain()

    loads = [
        pltpu.make_async_copy(ca, xa.at[pl.ds(0, 256)], ld.at[0]),
        pltpu.make_async_copy(qa, xa.at[pl.ds(256, 64)], ld.at[1]),
        pltpu.make_async_copy(ei, eib, ld.at[2]),
        pltpu.make_async_copy(cg, xg.at[pl.ds(0, 256)], ld.at[3]),
        pltpu.make_async_copy(qg, xg.at[pl.ds(256, 64)], ld.at[4]),
    ]

    def eo_load(g):
        return pltpu.make_async_copy(eo.at[:, pl.ds(pl.multiple_of(g * 256, 256), 256)], eob.at[g], ld.at[5 + g])

    def ev_load(g):
        row = pl.multiple_of((2 * g + tok) * 128, 128)
        return pltpu.make_async_copy(ev.at[pl.ds(row, 128)], evb.at[g], evs.at[g])

    for load in loads:
        load.start()
    for g in range(GROUPS):
        eo_load(g).start()

    barrier = pltpu.get_barrier_semaphore()

    def greet(r):
        pl.semaphore_signal(barrier, inc=1, device_id=line_peer(r), device_id_type=MESH)
        pl.semaphore_signal(barrier, inc=1, device_id=plane_peer(r), device_id_type=MESH)

    each(greet)
    for g in range(GROUPS):
        ev_load(g).start()

    for load in loads[:3]:
        load.wait()
    apart = jnp.dot(xa[...], eib[...], preferred_element_type=F32)
    apc[...] = apart[:256].astype(BF16)
    apq[...] = apart[256:]

    for load in loads[3:]:
        load.wait()
    gpq[:, 1, :, 384:] = jnp.zeros((2, 64, 128), BF16)

    def rotate(g):
        eo_load(g).wait()
        part = jnp.dot(xg[...], eob[g], preferred_element_type=F32).astype(BF16)
        for t in range(2):
            gpc[t, :, g * 128:(g + 1) * 128] = part[:256, t * 128:(t + 1) * 128]
            gpq[t, g // 4, :, (g % 4) * 128:(g % 4 + 1) * 128] = part[256:, t * 128:(t + 1) * 128]

    def c_rows(owner):
        return pl.ds(pl.multiple_of(lax.rem(owner + 16, 8) * 32, 32), 32)

    def q_rows(owner):
        return pl.ds(pl.multiple_of(lax.rem(owner + 16, 8) // 2 * 16, 16), 16)

    def q_cols(owner):
        return pl.ds(pl.multiple_of(lax.rem(owner + 16, 2) * 256, 256), 256)

    def own_part(kind, t, owner, cs):
        if kind == 0:
            return gpq.at[t, cs, q_rows(owner), q_cols(owner)]
        return gpc.at[t, c_rows(owner), pl.ds(*SETS[cs])]

    def slot(kind, d, s, t, cs):
        if kind == 0:
            return rsq.at[d, s - 1, t, cs]
        return rsc.at[d, s - 1, t, :, pl.ds(*SETS[cs])]

    def sign(d):
        return 1 if d == 0 else -1

    BOTH = slice(None)

    def rs_copies(kind, d, s, cs):
        first = 1 if cs == d else 2
        dz = 1 if d == 0 else 7
        if s < 4:
            if s == first:
                src = own_part(kind, BOTH, z + sign(d) * (5 - s), cs)
            else:
                src = slot(kind, d, s - 1, BOTH, cs)
            return [remote(src, slot(kind, d, s, BOTH, cs), rs_s.at[kind, d, s - 1, cs],
                           rs_r.at[kind, d, s - 1, cs], dev(0, 0, 0, dz))]
        return [
            remote(slot(kind, d, 3, t, cs), slot(kind, d, 4, j, cs), rs_s.at[kind, d, 3 + j, cs],
                   rs_r.at[kind, d, 3 + j, cs], dev(2 * j, 0, 0, dz))
            for j, t in ((1, 1 - tok), (0, tok))
        ]

    def rs_send(kind, d, s, cs):
        send(("rs", kind, d, s, cs), several(rs_copies(kind, d, s, cs)))

    def rs_step(kind, s):
        for n in range(2 if s > 1 else 1):
            for d in range(2):
                cs = d if n == 0 else 1 - d
                arrive(("rs", kind, d, s, cs))
                held = slot(kind, d, s, BOTH, cs)
                own = own_part(kind, BOTH, z + sign(d) * (4 - s), cs)
                held[...] = (held[...].astype(F32) + own[...].astype(F32)).astype(BF16)
                rs_send(kind, d, s + 1, cs)

    for g in range(4):
        rotate(g)
    pl.semaphore_wait(barrier, 30)
    for kind in range(2):
        rs_send(kind, 0, 1, 0)
        rs_send(kind, 1, 2, 0)
    other = pl.ds(pl.multiple_of((1 - c) * 512, 512), 512)
    mine = pl.ds(pl.multiple_of(c * 512, 512), 512)
    send("core 1", several([
        remote(apc.at[:, other], rac, co_s.at[0], co_r.at[0], dev(0, 0, 1, 0)),
        remote(apq.at[:, other], raq, co_s.at[1], co_r.at[1], dev(0, 0, 1, 0)),
    ]))
    for g in range(4, 7):
        rotate(g)
    for kind in range(2):
        rs_send(kind, 1, 1, 1)
        rs_send(kind, 0, 2, 1)
    send("own", several([
        remote(gpq.at[1 - tok, :, q_rows(z), q_cols(z)], oxq, co_s.at[4], co_r.at[4], dev(2, 0, 0, 0)),
        remote(gpc.at[1 - tok, c_rows(z)], oxc, co_s.at[5], co_r.at[5], dev(2, 0, 0, 0)),
    ]))

    arrive("core 1")
    rac[...] = (rac[...].astype(F32) + apc[:, mine].astype(F32)).astype(BF16)
    raq[...] = raq[...] + apq[:, mine]

    def a_scatter(r):
        dx, dy = plane_shift(r)
        nx = lax.rem(x + dx, 4)
        cols = pl.ds(pl.multiple_of(lax.rem(y + dy, 4) * 128, 128), 128)
        return (
            remote(rac.at[pl.ds(pl.multiple_of(nx * 64, 64), 64), cols], rdc.at[chip],
                   pr_s.at[0, r], pr_r.at[0, r], plane_peer(r)),
            remote(raq.at[pl.ds(pl.multiple_of(nx * 16, 16), 16), cols], rdq.at[chip],
                   pr_s.at[1, r], pr_r.at[1, r], plane_peer(r)),
        )

    send("scatter", bundle(a_scatter))
    own_rows_c = pl.ds(pl.multiple_of(x * 64, 64), 64)
    own_rows_q = pl.ds(pl.multiple_of(x * 16, 16), 16)
    own_cols = pl.ds(pl.multiple_of(y * 128, 128), 128)
    rdc[chip] = rac[own_rows_c, own_cols]
    rdq[chip] = raq[own_rows_q, own_cols]

    for kind in range(2):
        rs_step(kind, 1)

    total = jnp.zeros((8, 128), F32)
    for g in range(GROUPS):
        ev_load(g).wait()
        for cb in range(8):
            vals = evb[g, :, cb * 128:(cb + 1) * 128].astype(F32)
            total = total + jnp.sum(vals.reshape(16, 8, 128), axis=0)

    def all_to(buf, place, kind, peer):
        def body(r):
            return [remote(buf.at[place], buf.at[place], st_s.at[kind, r], st_r.at[kind, r], peer(r))]
        return bundle(body)

    ea[line] = jnp.sum(total, axis=0, keepdims=True)
    send("e line", all_to(ea, line, 0, line_peer))

    for kind in range(2):
        rs_step(kind, 2)

    arrive("e line")
    eb[chip] = jnp.sum(ea[...], axis=0)
    send("e plane", all_to(eb, chip, 1, plane_peer))

    arrive("scatter")
    piece_cols = pl.ds(pl.multiple_of(c * 512 + y * 128, 128), 128)
    afc[own_rows_c, piece_cols] = jnp.sum(rdc[...].astype(F32), axis=0).astype(BF16)
    afq[own_rows_q, piece_cols] = jnp.sum(rdq[...], axis=0).astype(BF16)

    def a_gather(r):
        return (
            remote(afc.at[own_rows_c, piece_cols], afc.at[own_rows_c, piece_cols],
                   pr_s.at[2, r], pr_r.at[2, r], plane_peer(r)),
            remote(afq.at[own_rows_q, piece_cols], afq.at[own_rows_q, piece_cols],
                   pr_s.at[3, r], pr_r.at[3, r], plane_peer(r)),
        )

    send("gather", bundle(a_gather))

    for kind in range(2):
        rs_step(kind, 3)

    arrive("own")

    def full_part(kind, owner, cs):
        if kind == 0:
            return gfq.at[cs, q_rows(owner), q_cols(owner)]
        return gfc.at[c_rows(owner), pl.ds(*SETS[cs])]

    def ag_copy(kind, d, s, cs):
        part = full_part(kind, z - sign(d) * (s - 1), cs)
        return remote(part, part, ag_s.at[kind, d, s - 1, cs], ag_r.at[kind, d, s - 1, cs],
                      dev(0, 0, 0, 1 if d == 0 else 7))

    def ag_send(kind, d, s, cs):
        send(("ag", kind, d, s, cs), single(ag_copy(kind, d, s, cs)))

    def owner_sum(kind):
        for cs in range(2):
            arrive(("rs", kind, 0, 4, cs))
            arrive(("rs", kind, 1, 4, cs))
            value = own_part(kind, tok, z, cs)[...].astype(F32)
            value = value + (oxq[cs] if kind == 0 else oxc[:, pl.ds(*SETS[cs])]).astype(F32)
            for d in range(2):
                for j in range(2):
                    value = value + slot(kind, d, 4, j, cs)[...].astype(F32)
            full_part(kind, z, cs)[...] = value.astype(BF16)
            for d in range(2):
                ag_send(kind, d, 1, cs)

    owner_sum(0)
    owner_sum(1)

    arrive("e plane")
    eigen_sum = jnp.sum(jnp.sum(eb[...], axis=0))
    damping = 0.1 * eigen_sum / (FF * D)

    def invert(g, carry):
        inv[g] = 1.0 / (evb[g].astype(F32) + damping)
        return carry

    lax.fori_loop(0, GROUPS, invert, 0)

    def ag_step(kind, s):
        for n in range(2 if s < 4 else 1):
            for d in range(2):
                cs = d if n == 0 else 1 - d
                arrive(("ag", kind, d, s, cs))
                if s < 3 or (s == 3 and cs == d):
                    ag_send(kind, d, s + 1, cs)

    ag_step(0, 1)
    arrive("gather")
    send("core 2", several([
        remote(afc.at[:, mine], afc.at[:, mine], co_s.at[2], co_r.at[2], dev(0, 0, 1, 0)),
        remote(afq.at[:, mine], afq.at[:, mine], co_s.at[3], co_r.at[3], dev(0, 0, 1, 0)),
    ]))
    ag_step(1, 1)

    ids = jnp.zeros((1, 64), jnp.int32)
    lane = lax.broadcasted_iota(jnp.int32, (1, 64), 1)
    for s in range(64):
        ids = jnp.where(lane == s, qi[s], ids)
    doc = lax.broadcasted_iota(jnp.int32, (16, 256), 0)
    position = lax.broadcasted_iota(jnp.int32, (16, 256), 1)
    first = jnp.zeros((16, 256), jnp.int32)
    last = jnp.zeros((16, 256), jnp.int32)
    start = jnp.int32(0)
    for n in range(16):
        stop = start + dl[n]
        first = jnp.where(doc == n, start, first)
        last = jnp.where(doc == n, stop, last)
        start = stop
    member = ((position >= first) & (position < last)).astype(F32)

    ag_step(0, 2)
    ag_step(1, 2)
    ag_step(0, 3)
    arrive("core 2")
    ag_step(0, 4)

    def contract(g, carry):
        cols = pl.ds(pl.multiple_of(lax.rem(g, 4) * 128, 128), 128)
        turned = gfq[g // 4, :, cols].astype(F32).T
        stacked = jnp.concatenate(
            [jnp.where(ids == q, turned, 0.0).astype(BF16) for q in range(Q)], axis=0
        )
        outer = jnp.dot(stacked, afq[...], preferred_element_type=F32)
        scale = inv[g]
        precond = jnp.concatenate(
            [(scale * outer[q * 128:(q + 1) * 128]).astype(BF16) for q in range(Q)], axis=0
        )
        mm[g] = lax.dot_general(
            afc[...], precond, (((1,), (1,)), ((), ())), preferred_element_type=F32
        )
        return carry

    lax.fori_loop(0, 2, contract, 0)
    ag_step(1, 3)
    lax.fori_loop(2, GROUPS, contract, 0)
    ag_step(1, 4)

    columns = []
    for q in range(Q):
        acc = jnp.zeros((256, 128), F32)
        for g in range(GROUPS):
            acc = acc + gfc[:, g * 128:(g + 1) * 128].astype(F32) * mm[g, :, q * 128:(q + 1) * 128]
        columns.append(acc)
    spread = jnp.dot(
        member, jnp.concatenate(columns, axis=1), precision=lax.Precision.HIGHEST, preferred_element_type=F32
    )
    column = lax.broadcasted_iota(jnp.int32, (16, 128), 1) - Q * lax.broadcasted_iota(jnp.int32, (16, 128), 0)
    scores = jnp.zeros((16, 128), F32)
    for q in range(Q):
        value = jnp.sum(spread[:, q * 128:(q + 1) * 128], axis=1, keepdims=True)
        scores = jnp.where(column == q, value, scores)
    fa[line] = jnp.sum(scores, axis=0, keepdims=True)
    early = list(sends)
    sends.clear()
    send("f line", all_to(fa, line, 2, line_peer))
    late = list(sends)
    sends[:] = early
    drain()
    arrive("f line")
    fb[chip] = jnp.sum(fa[...], axis=0)
    send("f plane", all_to(fb, chip, 3, plane_peer))
    arrive("f plane")
    whole = jnp.broadcast_to(jnp.sum(fb[...], axis=0), (16, 128))
    place = lax.broadcasted_iota(jnp.int32, (16, Q), 1)
    result = jnp.zeros((16, Q), F32)
    for q in range(Q):
        value = jnp.sum(jnp.where(column == q, whole, 0.0), axis=1, keepdims=True)
        result = jnp.where(place == q, value, result)
    out[...] = result
    sends.extend(late)
    finish()


def local(*args):
    dma = pltpu.SemaphoreType.DMA
    vm = pltpu.VMEM
    return pl.pallas_call(
        kernel,
        out_shape=jax.ShapeDtypeStruct((16, Q), F32),
        in_specs=[pl.BlockSpec(memory_space=pl.ANY)] * 7 + [pl.BlockSpec(memory_space=pltpu.SMEM)] * 2,
        out_specs=pl.BlockSpec(memory_space=pltpu.VMEM),
        scratch_shapes=[
            vm((320, 1792), BF16), vm((320, 256), BF16), vm((GROUPS, 1792, 256), BF16), vm((256, 1024), BF16),
            vm((GROUPS, 128, 1024), BF16),
            vm((2, 256, 896), BF16), vm((2, 2, 64, 512), BF16),
            vm((2, 4, 2, 32, 896), BF16), vm((2, 4, 2, 2, 16, 256), BF16),
            vm((32, 896), BF16), vm((2, 16, 256), BF16),
            vm((256, 896), BF16), vm((2, 64, 512), BF16),
            vm((256, 1024), BF16), vm((64, 1024), F32),
            vm((256, 512), BF16), vm((64, 512), F32),
            vm((16, 64, 128), BF16), vm((16, 16, 128), F32),
            vm((256, 1024), BF16), vm((64, 1024), BF16),
            vm((GROUPS, 128, 1024), F32), vm((GROUPS, 256, 512), F32),
            vm((16, 1, 128), F32), vm((16, 1, 128), F32), vm((16, 1, 128), F32), vm((16, 1, 128), F32),
            dma((5 + GROUPS,)), dma((GROUPS,)),
            dma((2, 2, 5, 2)), dma((2, 2, 5, 2)),
            dma((2, 2, 4, 2)), dma((2, 2, 4, 2)),
            dma((6,)), dma((6,)),
            dma((4, 16)), dma((4, 16)),
            dma((4, 16)), dma((4, 16)),
        ],
        name="influence",
        compiler_params=pltpu.CompilerParams(
            collective_id=0, has_side_effects=True, vmem_limit_bytes=63 << 20
        ),
    )(*args)


def solution(mesh):
    in_specs = (
        P(None, ("tok", "inp")),
        P(None, ("tok", "out")),
        P(None, ("tok", "inp")),
        P(None, ("tok", "out")),
        P(("tok", "inp"), "out"),
        P(("tok", "out"), "inp"),
        P("out", "inp"),
        P(),
        P(),
    )
    return jax.shard_map(local, mesh=mesh, in_specs=in_specs, out_specs=P(), check_vma=False)
```

```python
import jax
import jax.numpy as jnp
from jax import lax
from jax.experimental import pallas as pl
from jax.experimental.pallas import tpu as pltpu
from jax.sharding import PartitionSpec as P

D = 8192
FF = 28672
Q = 4
MESH = pl.DeviceIdType.MESH
F32 = jnp.float32
BF16 = jnp.bfloat16
GROUPS = 7
SETS = ((0, 512), (512, 384))


def kernel(
    cg, ca, qg, qa, eo, ei, ev, dl, qi, out,
    xg, xa, eob, eib, evb, gpc, gpq, rsc, rsq, oxc, oxq, gfc, gfq,
    apc, apq, rac, raq, rdc, rdq, afc, afq, inv, mm, ea, eb, fa, fb,
    ld, evs, rs_s, rs_r, ag_s, ag_r, co_s, co_r, pr_s, pr_r, st_s, st_r,
):
    tok, o, z = lax.axis_index("tok"), lax.axis_index("out"), lax.axis_index("inp")
    x = tok * 2 + o // 8
    y = lax.rem(o // 2, 4)
    c = lax.rem(o, 2)
    chip = x * 4 + y
    line = c * 8 + z

    def dev(dx, dy, dc, dz):
        nx = lax.rem(x + dx, 4)
        ny = lax.rem(y + dy, 4)
        nc = lax.rem(c + dc, 2)
        return (nx // 2, lax.rem(nx, 2) * 8 + ny * 2 + nc, lax.rem(z + dz, 8))

    def remote(src, dst, ss, rs, where):
        return pltpu.make_async_remote_copy(
            src_ref=src, dst_ref=dst, send_sem=ss, recv_sem=rs, device_id=where, device_id_type=MESH
        )

    def line_peer(r):
        n = r - 1 + r // 15
        j = n // 2
        odd = lax.rem(j, 2)
        dz = 4 + odd * ((j + 1) // 2) + (1 - odd) * (8 - j // 2)
        return dev(0, 0, lax.rem(n, 2), dz)

    def plane_shift(r):
        n = r - 1 + r // 11
        return lax.rem(2 + n // 4, 4), lax.rem(2 + lax.rem(n, 4), 4)

    def plane_peer(r):
        dx, dy = plane_shift(r)
        return dev(dx, dy, 0, 0)

    def each(body):
        lax.fori_loop(1, 16, lambda r, carry: (body(r), carry)[1], 0)

    waits, sends = {}, {}

    def send(key, start, arrivals, departures):
        start()
        waits[key] = arrivals
        for name, leave in departures.items():
            sends.setdefault(name, []).append(leave)

    def arrive(key):
        for copy in waits.pop(key):
            copy.wait_recv()

    def drain():
        for leaves in sends.values():
            leaves[0](len(leaves)).wait_send()
        sends.clear()

    def finish():
        for key in list(waits):
            arrive(key)
        drain()

    def sized(ref, ss, rs):
        return remote(ref, ref, ss, rs, dev(0, 0, 1, 0))

    def post(key, copies):
        def start():
            for copy in copies:
                copy.start()
        send(key, start, copies, {(key, n): (lambda count, copy=copy: copy) for n, copy in enumerate(copies)})

    def exchange(key, copies, whole):
        def start():
            def body(r):
                for copy in copies(r):
                    copy.start()
            each(body)
        send(key, start, whole, {(key, n): (lambda count, copy=copy: copy) for n, copy in enumerate(whole)})

    loads = [
        pltpu.make_async_copy(ca, xa.at[pl.ds(0, 256)], ld.at[0]),
        pltpu.make_async_copy(qa, xa.at[pl.ds(256, 64)], ld.at[1]),
        pltpu.make_async_copy(ei, eib, ld.at[2]),
        pltpu.make_async_copy(cg, xg.at[pl.ds(0, 256)], ld.at[3]),
        pltpu.make_async_copy(qg, xg.at[pl.ds(256, 64)], ld.at[4]),
    ]

    def eo_load(g):
        return pltpu.make_async_copy(eo.at[:, pl.ds(pl.multiple_of(g * 256, 256), 256)], eob.at[g], ld.at[5 + g])

    def ev_load(g):
        row = pl.multiple_of((2 * g + tok) * 128, 128)
        return pltpu.make_async_copy(ev.at[pl.ds(row, 128)], evb.at[g], evs.at[0])

    for load in loads:
        load.start()
    for g in range(GROUPS):
        eo_load(g).start()

    barrier = pltpu.get_barrier_semaphore()

    def greet(r):
        pl.semaphore_signal(barrier, inc=1, device_id=line_peer(r), device_id_type=MESH)
        pl.semaphore_signal(barrier, inc=1, device_id=plane_peer(r), device_id_type=MESH)

    each(greet)
    for g in range(GROUPS):
        ev_load(g).start()

    for load in loads[:3]:
        load.wait()
    apart = jnp.dot(xa[...], eib[...], preferred_element_type=F32)
    apc[...] = apart[:256].astype(BF16)
    apq[...] = apart[256:]

    for load in loads[3:]:
        load.wait()
    gpq[:, 1, :, 384:] = jnp.zeros((2, 64, 128), BF16)

    def rotate(g):
        eo_load(g).wait()
        part = jnp.dot(xg[...], eob[g], preferred_element_type=F32).astype(BF16)
        for t in range(2):
            gpc[t, :, g * 128:(g + 1) * 128] = part[:256, t * 128:(t + 1) * 128]
            gpq[t, g // 4, :, (g % 4) * 128:(g % 4 + 1) * 128] = part[256:, t * 128:(t + 1) * 128]

    def c_rows(owner):
        return pl.ds(pl.multiple_of(lax.rem(owner + 16, 8) * 32, 32), 32)

    def q_rows(owner):
        return pl.ds(pl.multiple_of(lax.rem(owner + 16, 8) // 2 * 16, 16), 16)

    def q_cols(owner):
        return pl.ds(pl.multiple_of(lax.rem(owner + 16, 2) * 256, 256), 256)

    def own_part(kind, t, owner, cs):
        if kind == 0:
            return gpq.at[t, cs, q_rows(owner), q_cols(owner)]
        return gpc.at[t, c_rows(owner), pl.ds(*SETS[cs])]

    def slot(kind, d, s, t, cs):
        if kind == 0:
            return rsq.at[d, s - 1, t, cs]
        return rsc.at[d, s - 1, t, :, pl.ds(*SETS[cs])]

    def sign(d):
        return 1 if d == 0 else -1

    BOTH = slice(None)

    def rs_copies(kind, d, s, cs):
        ss, rs = rs_s.at[kind, d, cs], rs_r.at[kind, d, s - 1, cs]
        first = 1 if cs == d else 2
        dz = 1 if d == 0 else 7
        if s < 4:
            if s == first:
                src = own_part(kind, BOTH, z + sign(d) * (5 - s), cs)
            else:
                src = slot(kind, d, s - 1, BOTH, cs)
            return [remote(src, slot(kind, d, s, BOTH, cs), ss, rs, dev(0, 0, 0, dz))]
        return [
            remote(slot(kind, d, 3, t, cs), slot(kind, d, 4, j, cs), ss, rs, dev(2 * j, 0, 0, dz))
            for j, t in ((1, 1 - tok), (0, tok))
        ]

    def rs_send(kind, d, s, cs):
        def start():
            for copy in rs_copies(kind, d, s, cs):
                copy.start()

        def leave(count):
            if kind == 0:
                return sized(rsq.at[d, pl.ds(0, count), :, cs], rs_s.at[kind, d, cs], rs_r.at[kind, d, 0, cs])
            return sized(rsc.at[d, pl.ds(0, count), :, :, pl.ds(*SETS[cs])], rs_s.at[kind, d, cs],
                         rs_r.at[kind, d, 0, cs])

        whole = sized(slot(kind, d, s, BOTH, cs), rs_s.at[kind, d, cs], rs_r.at[kind, d, s - 1, cs])
        send(("rs", kind, d, s, cs), start, [whole], {("rs", kind, d, cs): leave})

    def rs_step(kind, s):
        for n in range(2 if s > 1 else 1):
            for d in range(2):
                cs = d if n == 0 else 1 - d
                arrive(("rs", kind, d, s, cs))
                held = slot(kind, d, s, BOTH, cs)
                own = own_part(kind, BOTH, z + sign(d) * (4 - s), cs)
                held[...] = (held[...].astype(F32) + own[...].astype(F32)).astype(BF16)
                rs_send(kind, d, s + 1, cs)

    for g in range(4):
        rotate(g)
    pl.semaphore_wait(barrier, 30)
    for kind in range(2):
        rs_send(kind, 0, 1, 0)
        rs_send(kind, 1, 2, 0)
    other = pl.ds(pl.multiple_of((1 - c) * 512, 512), 512)
    mine = pl.ds(pl.multiple_of(c * 512, 512), 512)
    post("core 1", [
        remote(apc.at[:, other], rac, co_s.at[0], co_r.at[0], dev(0, 0, 1, 0)),
        remote(apq.at[:, other], raq, co_s.at[1], co_r.at[1], dev(0, 0, 1, 0)),
    ])
    for g in range(4, 7):
        rotate(g)
    for kind in range(2):
        rs_send(kind, 1, 1, 1)
        rs_send(kind, 0, 2, 1)
    post("own", [
        remote(gpq.at[1 - tok, :, q_rows(z), q_cols(z)], oxq, co_s.at[4], co_r.at[4], dev(2, 0, 0, 0)),
        remote(gpc.at[1 - tok, c_rows(z)], oxc, co_s.at[5], co_r.at[5], dev(2, 0, 0, 0)),
    ])

    arrive("core 1")
    rac[...] = (rac[...].astype(F32) + apc[:, mine].astype(F32)).astype(BF16)
    raq[...] = raq[...] + apq[:, mine]

    def a_scatter(r):
        dx, dy = plane_shift(r)
        nx = lax.rem(x + dx, 4)
        cols = pl.ds(pl.multiple_of(lax.rem(y + dy, 4) * 128, 128), 128)
        return (
            remote(rac.at[pl.ds(pl.multiple_of(nx * 64, 64), 64), cols], rdc.at[chip],
                   pr_s.at[0], pr_r.at[0], plane_peer(r)),
            remote(raq.at[pl.ds(pl.multiple_of(nx * 16, 16), 16), cols], rdq.at[chip],
                   pr_s.at[1], pr_r.at[1], plane_peer(r)),
        )

    exchange("scatter", a_scatter, [
        sized(rdc.at[pl.ds(0, 15)], pr_s.at[0], pr_r.at[0]),
        sized(rdq.at[pl.ds(0, 15)], pr_s.at[1], pr_r.at[1]),
    ])
    own_rows_c = pl.ds(pl.multiple_of(x * 64, 64), 64)
    own_rows_q = pl.ds(pl.multiple_of(x * 16, 16), 16)
    own_cols = pl.ds(pl.multiple_of(y * 128, 128), 128)
    rdc[chip] = rac[own_rows_c, own_cols]
    rdq[chip] = raq[own_rows_q, own_cols]

    for kind in range(2):
        rs_step(kind, 1)

    total = jnp.zeros((8, 128), F32)
    pltpu.make_async_copy(evb, evb, evs.at[0]).wait()
    for g in range(GROUPS):
        for cb in range(8):
            vals = evb[g, :, cb * 128:(cb + 1) * 128].astype(F32)
            total = total + jnp.sum(vals.reshape(16, 8, 128), axis=0)

    def all_to(key, buf, place, kind, peer):
        def body(r):
            return [remote(buf.at[place], buf.at[place], st_s.at[kind], st_r.at[kind], peer(r))]
        exchange(key, body, [sized(buf.at[pl.ds(0, 15)], st_s.at[kind], st_r.at[kind])])

    ea[line] = jnp.sum(total, axis=0, keepdims=True)
    all_to("e line", ea, line, 0, line_peer)

    for kind in range(2):
        rs_step(kind, 2)

    arrive("e line")
    eb[chip] = jnp.sum(ea[...], axis=0)
    all_to("e plane", eb, chip, 1, plane_peer)

    for kind in range(2):
        rs_step(kind, 3)

    arrive("scatter")
    piece_cols = pl.ds(pl.multiple_of(c * 512 + y * 128, 128), 128)
    afc[own_rows_c, piece_cols] = jnp.sum(rdc[...].astype(F32), axis=0).astype(BF16)
    afq[own_rows_q, piece_cols] = jnp.sum(rdq[...], axis=0).astype(BF16)

    def a_gather(r):
        return (
            remote(afc.at[own_rows_c, piece_cols], afc.at[own_rows_c, piece_cols],
                   pr_s.at[2], pr_r.at[2], plane_peer(r)),
            remote(afq.at[own_rows_q, piece_cols], afq.at[own_rows_q, piece_cols],
                   pr_s.at[3], pr_r.at[3], plane_peer(r)),
        )

    exchange("gather", a_gather, [
        sized(afc.at[pl.ds(0, 240), pl.ds(0, 512)], pr_s.at[2], pr_r.at[2]),
        sized(afq.at[pl.ds(0, 48), pl.ds(0, 640)], pr_s.at[3], pr_r.at[3]),
    ])

    arrive("own")

    def full_part(kind, owner, cs):
        if kind == 0:
            return gfq.at[cs, q_rows(owner), q_cols(owner)]
        return gfc.at[c_rows(owner), pl.ds(*SETS[cs])]

    def ag_copy(kind, d, s, cs):
        part = full_part(kind, z - sign(d) * (s - 1), cs)
        return remote(part, part, ag_s.at[kind, d, cs], ag_r.at[kind, d, s - 1, cs],
                      dev(0, 0, 0, 1 if d == 0 else 7))

    def ag_send(kind, d, s, cs):
        copy = ag_copy(kind, d, s, cs)

        def leave(count):
            if kind == 0:
                ref = gfq.at[cs, pl.ds(0, 16 * count), pl.ds(0, 256)]
            else:
                ref = gfc.at[pl.ds(0, 32 * count), pl.ds(*SETS[cs])]
            return sized(ref, ag_s.at[kind, d, cs], ag_r.at[kind, d, 0, cs])

        send(("ag", kind, d, s, cs), copy.start, [copy], {("ag", kind, d, cs): leave})

    def owner_sum(kind):
        for cs in range(2):
            arrive(("rs", kind, 0, 4, cs))
            arrive(("rs", kind, 1, 4, cs))
            value = own_part(kind, tok, z, cs)[...].astype(F32)
            value = value + (oxq[cs] if kind == 0 else oxc[:, pl.ds(*SETS[cs])]).astype(F32)
            for d in range(2):
                for j in range(2):
                    value = value + slot(kind, d, 4, j, cs)[...].astype(F32)
            full_part(kind, z, cs)[...] = value.astype(BF16)
            for d in range(2):
                ag_send(kind, d, 1, cs)

    owner_sum(0)
    owner_sum(1)

    arrive("e plane")
    eigen_sum = jnp.sum(jnp.sum(eb[...], axis=0))
    damping = 0.1 * eigen_sum / (FF * D)

    def invert(g, carry):
        inv[g] = 1.0 / (evb[g].astype(F32) + damping)
        return carry

    lax.fori_loop(0, GROUPS, invert, 0)

    def ag_step(kind, s):
        for n in range(2 if s < 4 else 1):
            for d in range(2):
                cs = d if n == 0 else 1 - d
                arrive(("ag", kind, d, s, cs))
                if s < 3 or (s == 3 and cs == d):
                    ag_send(kind, d, s + 1, cs)

    ag_step(0, 1)
    arrive("gather")
    post("core 2", [
        remote(afc.at[:, mine], afc.at[:, mine], co_s.at[2], co_r.at[2], dev(0, 0, 1, 0)),
        remote(afq.at[:, mine], afq.at[:, mine], co_s.at[3], co_r.at[3], dev(0, 0, 1, 0)),
    ])
    ag_step(1, 1)

    ids = jnp.zeros((1, 64), jnp.int32)
    lane = lax.broadcasted_iota(jnp.int32, (1, 64), 1)
    for s in range(64):
        ids = jnp.where(lane == s, qi[s], ids)
    doc = lax.broadcasted_iota(jnp.int32, (16, 256), 0)
    position = lax.broadcasted_iota(jnp.int32, (16, 256), 1)
    first = jnp.zeros((16, 256), jnp.int32)
    last = jnp.zeros((16, 256), jnp.int32)
    start = jnp.int32(0)
    for n in range(16):
        stop = start + dl[n]
        first = jnp.where(doc == n, start, first)
        last = jnp.where(doc == n, stop, last)
        start = stop
    member = ((position >= first) & (position < last)).astype(F32)

    ag_step(0, 2)
    ag_step(1, 2)
    ag_step(0, 3)
    arrive("core 2")
    ag_step(0, 4)

    def contract(g, carry):
        cols = pl.ds(pl.multiple_of(lax.rem(g, 4) * 128, 128), 128)
        turned = gfq[g // 4, :, cols].astype(F32).T
        stacked = jnp.concatenate(
            [jnp.where(ids == q, turned, 0.0).astype(BF16) for q in range(Q)], axis=0
        )
        outer = jnp.dot(stacked, afq[...], preferred_element_type=F32)
        scale = inv[g]
        precond = jnp.concatenate(
            [(scale * outer[q * 128:(q + 1) * 128]).astype(BF16) for q in range(Q)], axis=0
        )
        mm[g] = lax.dot_general(
            afc[...], precond, (((1,), (1,)), ((), ())), preferred_element_type=F32
        )
        return carry

    lax.fori_loop(0, 2, contract, 0)
    ag_step(1, 3)
    lax.fori_loop(2, GROUPS, contract, 0)
    ag_step(1, 4)

    columns = []
    for q in range(Q):
        acc = jnp.zeros((256, 128), F32)
        for g in range(GROUPS):
            acc = acc + gfc[:, g * 128:(g + 1) * 128].astype(F32) * mm[g, :, q * 128:(q + 1) * 128]
        columns.append(acc)
    spread = jnp.dot(
        member, jnp.concatenate(columns, axis=1), precision=lax.Precision.HIGHEST, preferred_element_type=F32
    )
    column = lax.broadcasted_iota(jnp.int32, (16, 128), 1) - Q * lax.broadcasted_iota(jnp.int32, (16, 128), 0)
    scores = jnp.zeros((16, 128), F32)
    for q in range(Q):
        value = jnp.sum(spread[:, q * 128:(q + 1) * 128], axis=1, keepdims=True)
        scores = jnp.where(column == q, value, scores)
    fa[line] = jnp.sum(scores, axis=0, keepdims=True)
    early = dict(sends)
    sends.clear()
    all_to("f line", fa, line, 2, line_peer)
    late = dict(sends)
    sends.clear()
    sends.update(early)
    drain()
    sends.update(late)
    arrive("f line")
    fb[chip] = jnp.sum(fa[...], axis=0)
    all_to("f plane", fb, chip, 3, plane_peer)
    arrive("f plane")
    whole = jnp.broadcast_to(jnp.sum(fb[...], axis=0), (16, 128))
    place = lax.broadcasted_iota(jnp.int32, (16, Q), 1)
    result = jnp.zeros((16, Q), F32)
    for q in range(Q):
        value = jnp.sum(jnp.where(column == q, whole, 0.0), axis=1, keepdims=True)
        result = jnp.where(place == q, value, result)
    out[...] = result
    finish()


def local(*args):
    dma = pltpu.SemaphoreType.DMA
    vm = pltpu.VMEM
    return pl.pallas_call(
        kernel,
        out_shape=jax.ShapeDtypeStruct((16, Q), F32),
        in_specs=[pl.BlockSpec(memory_space=pl.ANY)] * 7 + [pl.BlockSpec(memory_space=pltpu.SMEM)] * 2,
        out_specs=pl.BlockSpec(memory_space=pltpu.VMEM),
        scratch_shapes=[
            vm((320, 1792), BF16), vm((320, 256), BF16), vm((GROUPS, 1792, 256), BF16), vm((256, 1024), BF16),
            vm((GROUPS, 128, 1024), BF16),
            vm((2, 256, 896), BF16), vm((2, 2, 64, 512), BF16),
            vm((2, 4, 2, 32, 896), BF16), vm((2, 4, 2, 2, 16, 256), BF16),
            vm((32, 896), BF16), vm((2, 16, 256), BF16),
            vm((256, 896), BF16), vm((2, 64, 512), BF16),
            vm((256, 1024), BF16), vm((64, 1024), F32),
            vm((256, 512), BF16), vm((64, 512), F32),
            vm((16, 64, 128), BF16), vm((16, 16, 128), F32),
            vm((256, 1024), BF16), vm((64, 1024), BF16),
            vm((GROUPS, 128, 1024), F32), vm((GROUPS, 256, 512), F32),
            vm((16, 1, 128), F32), vm((16, 1, 128), F32), vm((16, 1, 128), F32), vm((16, 1, 128), F32),
            dma((5 + GROUPS,)), dma((1,)),
            dma((2, 2, 2)), dma((2, 2, 4, 2)),
            dma((2, 2, 2)), dma((2, 2, 4, 2)),
            dma((6,)), dma((6,)),
            dma((4,)), dma((4,)),
            dma((4,)), dma((4,)),
        ],
        name="influence",
        compiler_params=pltpu.CompilerParams(
            collective_id=0, has_side_effects=True, vmem_limit_bytes=63 << 20
        ),
    )(*args)


def solution(mesh):
    in_specs = (
        P(None, ("tok", "inp")),
        P(None, ("tok", "out")),
        P(None, ("tok", "inp")),
        P(None, ("tok", "out")),
        P(("tok", "inp"), "out"),
        P(("tok", "out"), "inp"),
        P("out", "inp"),
        P(),
        P(),
    )
    return jax.shard_map(local, mesh=mesh, in_specs=in_specs, out_specs=P(), check_vma=False)
```

```python
import jax
import jax.numpy as jnp
from jax import lax
from jax.experimental import pallas as pl
from jax.experimental.pallas import tpu as pltpu
from jax.sharding import PartitionSpec as P

D = 8192
FF = 28672
Q = 4
MESH = pl.DeviceIdType.MESH
F32 = jnp.float32
BF16 = jnp.bfloat16
GROUPS = 7
SETS = ((0, 256), (256, 256), (512, 256), (768, 128))
ENDS = ((0, 512), (512, 384))


def kernel(
    cg, ca, qg, qa, eo, ei, ev, dl, qi, out,
    xg, xa, eob, eib, evb, gpc, gpq, rsc, rsq, oxc, oxq, gfc, gfq,
    apk, rap, rda, afa, inv, mm, ea, eb, fa, fb,
    ld, evs, rq_s, rq_r, rc_s, rc_r, ag_s, ag_r, co_s, co_r, pr_s, pr_r, st_s, st_r,
):
    tok, o, z = lax.axis_index("tok"), lax.axis_index("out"), lax.axis_index("inp")
    x = tok * 2 + o // 8
    y = lax.rem(o // 2, 4)
    c = lax.rem(o, 2)
    chip = x * 4 + y
    line = c * 8 + z

    def dev(dx, dy, dc, dz):
        nx = lax.rem(x + dx, 4)
        ny = lax.rem(y + dy, 4)
        nc = lax.rem(c + dc, 2)
        return (nx // 2, lax.rem(nx, 2) * 8 + ny * 2 + nc, lax.rem(z + dz, 8))

    def remote(src, dst, ss, rs, where):
        return pltpu.make_async_remote_copy(
            src_ref=src, dst_ref=dst, send_sem=ss, recv_sem=rs, device_id=where, device_id_type=MESH
        )

    def line_peer(r):
        n = r - 1 + r // 15
        j = n // 2
        odd = lax.rem(j, 2)
        dz = 4 + odd * ((j + 1) // 2) + (1 - odd) * (8 - j // 2)
        return dev(0, 0, lax.rem(n, 2), dz)

    def plane_shift(r):
        n = r - 1 + r // 11
        return lax.rem(2 + n // 4, 4), lax.rem(2 + lax.rem(n, 4), 4)

    def plane_peer(r):
        dx, dy = plane_shift(r)
        return dev(dx, dy, 0, 0)

    def each(body):
        lax.fori_loop(1, 16, lambda r, carry: (body(r), carry)[1], 0)

    waits, sends = {}, {}

    def send(key, start, arrivals, departures):
        start()
        waits[key] = arrivals
        for name, leave in departures.items():
            sends.setdefault(name, []).append(leave)

    def arrive(key):
        for copy in waits.pop(key):
            copy.wait_recv()

    def drain():
        for leaves in sends.values():
            leaves[0](len(leaves)).wait_send()
        sends.clear()

    def finish():
        for key in list(waits):
            arrive(key)
        drain()

    def sized(ref, ss, rs):
        return remote(ref, ref, ss, rs, dev(0, 0, 1, 0))

    def post(key, copies):
        def start():
            for copy in copies:
                copy.start()
        send(key, start, copies, {(key, n): (lambda count, copy=copy: copy) for n, copy in enumerate(copies)})

    def exchange(key, copies, whole):
        def start():
            def body(r):
                for copy in copies(r):
                    copy.start()
            each(body)
        send(key, start, whole, {(key, n): (lambda count, copy=copy: copy) for n, copy in enumerate(whole)})

    loads = [
        pltpu.make_async_copy(ca, xa.at[pl.ds(0, 256)], ld.at[0]),
        pltpu.make_async_copy(qa, xa.at[pl.ds(256, 64)], ld.at[1]),
        pltpu.make_async_copy(ei, eib, ld.at[2]),
        pltpu.make_async_copy(cg, xg.at[pl.ds(0, 256)], ld.at[3]),
        pltpu.make_async_copy(qg, xg.at[pl.ds(256, 64)], ld.at[4]),
    ]

    def eo_load(g):
        return pltpu.make_async_copy(eo.at[:, pl.ds(pl.multiple_of(g * 256, 256), 256)], eob.at[g], ld.at[5 + g])

    def ev_load(g):
        row = pl.multiple_of((2 * g + tok) * 128, 128)
        return pltpu.make_async_copy(ev.at[pl.ds(row, 128)], evb.at[g], evs.at[0])

    for load in loads:
        load.start()
    for g in range(GROUPS):
        eo_load(g).start()

    barrier = pltpu.get_barrier_semaphore()

    def greet(r):
        pl.semaphore_signal(barrier, inc=1, device_id=line_peer(r), device_id_type=MESH)
        pl.semaphore_signal(barrier, inc=1, device_id=plane_peer(r), device_id_type=MESH)

    each(greet)
    for g in range(GROUPS):
        ev_load(g).start()

    for load in loads[:3]:
        load.wait()
    apart = jnp.dot(xa[...], eib[...], preferred_element_type=F32)
    for i in range(4):
        apk[i, :64] = apart[i * 64:(i + 1) * 64]
        apk[i, 64:] = apart[256 + i * 16:256 + (i + 1) * 16]

    for load in loads[3:]:
        load.wait()
    gpq[:, 1, :, 384:] = jnp.zeros((2, 64, 128), F32)

    def rotate(g):
        eo_load(g).wait()
        part = jnp.dot(xg[...], eob[g], preferred_element_type=F32)
        for t in range(2):
            gpc[t, :, g * 128:(g + 1) * 128] = part[:256, t * 128:(t + 1) * 128].astype(BF16)
            gpq[t, g // 4, :, (g % 4) * 128:(g % 4 + 1) * 128] = part[256:, t * 128:(t + 1) * 128]

    def c_rows(owner):
        return pl.ds(pl.multiple_of(lax.rem(owner + 16, 8) * 32, 32), 32)

    def q_rows(owner):
        return pl.ds(pl.multiple_of(lax.rem(owner + 16, 8) // 2 * 16, 16), 16)

    def q_cols(owner):
        return pl.ds(pl.multiple_of(lax.rem(owner + 16, 2) * 256, 256), 256)

    def own_q(t, owner):
        return gpq.at[t, :, q_rows(owner), q_cols(owner)]

    def own_c(t, owner, cs):
        return gpc.at[t, c_rows(owner), pl.ds(*SETS[cs])]

    def sign(d):
        return 1 if d == 0 else -1

    BOTH = slice(None)

    def rs_q(d, s):
        ss, rs = rq_s.at[d], rq_r.at[d, s - 1]
        dz = 1 if d == 0 else 7
        if s < 4:
            src = own_q(BOTH, z + sign(d) * (5 - s)) if s == d + 1 else rsq.at[d, s - 2]
            copies = [remote(src, rsq.at[d, s - 1], ss, rs, dev(0, 0, 0, dz))]
        else:
            copies = [remote(rsq.at[d, 2, t], rsq.at[d, 3, j], ss, rs, dev(2 * j, 0, 0, dz))
                      for j, t in ((1, 1 - tok), (0, tok))]

        def start():
            for copy in copies:
                copy.start()

        send(("rq", d, s), start, [sized(rsq.at[d, s - 1], ss, rs)],
             {("rq", d): lambda count: sized(rsq.at[d, pl.ds(0, count)], ss, rs)})

    def slot(d, s, t, cs):
        return rsc.at[d, s - 1, t, :, pl.ds(*SETS[cs])]

    def rs_c(d, s, cs):
        ss, rs = rc_s.at[d, cs], rc_r.at[d, s - 1, cs]
        dz = 1 if d == 0 else 7
        first = 1 if cs % 2 == d else 2
        if s < 4:
            src = own_c(BOTH, z + sign(d) * (5 - s), cs) if s == first else slot(d, s - 1, BOTH, cs)
            copies = [remote(src, slot(d, s, BOTH, cs), ss, rs, dev(0, 0, 0, dz))]
        else:
            copies = [remote(slot(d, 3, t, cs), slot(d, 4, j, cs), ss, rs, dev(2 * j, 0, 0, dz))
                      for j, t in ((1, 1 - tok), (0, tok))]

        def start():
            for copy in copies:
                copy.start()

        send(("rc", d, s, cs), start, [sized(slot(d, s, BOTH, cs), ss, rs)],
             {("rc", d, cs): lambda count: sized(rsc.at[d, pl.ds(0, count), :, :, pl.ds(*SETS[cs])], ss, rs)})

    def add_to(held, own):
        held[...] = (held[...].astype(F32) + own[...].astype(F32)).astype(held.dtype)

    def rs_step(s):
        for d in range(2 if s > 1 else 1):
            arrive(("rq", d, s))
            add_to(rsq.at[d, s - 1], own_q(BOTH, z + sign(d) * (4 - s)))
            rs_q(d, s + 1)
        for cs in range(4):
            for d in ((cs % 2, 1 - cs % 2) if s > 1 else (cs % 2,)):
                arrive(("rc", d, s, cs))
                add_to(slot(d, s, BOTH, cs), own_c(BOTH, z + sign(d) * (4 - s), cs))
                rs_c(d, s + 1, cs)

    for g in range(4):
        rotate(g)
    pl.semaphore_wait(barrier, 30)
    for cs in range(2):
        rs_c(cs, 1, cs)
    for cs in range(2):
        rs_c(1 - cs, 2, cs)
    other = pl.ds(pl.multiple_of((1 - c) * 512, 512), 512)
    mine = pl.ds(pl.multiple_of(c * 512, 512), 512)
    post("core 1", [remote(apk.at[:, :, other], rap, co_s.at[0], co_r.at[0], dev(0, 0, 1, 0))])
    for g in range(4, 7):
        rotate(g)
    rs_q(0, 1)
    rs_q(1, 2)
    for cs in range(2, 4):
        rs_c(cs - 2, 1, cs)
    for cs in range(2, 4):
        rs_c(3 - cs, 2, cs)
    post("own", [
        remote(own_q(1 - tok, z), oxq, co_s.at[2], co_r.at[2], dev(2, 0, 0, 0)),
        remote(gpc.at[1 - tok, c_rows(z)], oxc, co_s.at[3], co_r.at[3], dev(2, 0, 0, 0)),
    ])

    arrive("core 1")
    rap[...] = rap[...] + apk[:, :, mine]

    def a_scatter(r):
        dx, dy = plane_shift(r)
        cols = pl.ds(pl.multiple_of(lax.rem(y + dy, 4) * 128, 128), 128)
        return [remote(rap.at[lax.rem(x + dx, 4), :, cols], rda.at[chip], pr_s.at[0], pr_r.at[0], plane_peer(r))]

    exchange("scatter", a_scatter, [sized(rda.at[pl.ds(0, 15)], pr_s.at[0], pr_r.at[0])])
    rda[chip] = rap[x, :, pl.ds(pl.multiple_of(y * 128, 128), 128)]

    rs_step(1)

    total = jnp.zeros((8, 128), F32)
    pltpu.make_async_copy(evb, evb, evs.at[0]).wait()
    for g in range(GROUPS):
        for cb in range(8):
            vals = evb[g, :, cb * 128:(cb + 1) * 128].astype(F32)
            total = total + jnp.sum(vals.reshape(16, 8, 128), axis=0)

    def all_to(key, buf, place, kind, peer):
        def body(r):
            return [remote(buf.at[place], buf.at[place], st_s.at[kind], st_r.at[kind], peer(r))]
        exchange(key, body, [sized(buf.at[pl.ds(0, 15)], st_s.at[kind], st_r.at[kind])])

    ea[line] = jnp.sum(total, axis=0, keepdims=True)
    all_to("e line", ea, line, 0, line_peer)

    rs_step(2)

    arrive("e line")
    eb[chip] = jnp.sum(ea[...], axis=0)
    all_to("e plane", eb, chip, 1, plane_peer)

    rs_step(3)

    arrive("scatter")
    piece_cols = pl.ds(pl.multiple_of(c * 512 + y * 128, 128), 128)
    afa[x, :, piece_cols] = jnp.sum(rda[...], axis=0).astype(BF16)

    def a_gather(r):
        ref = afa.at[x, :, piece_cols]
        return [remote(ref, ref, pr_s.at[1], pr_r.at[1], plane_peer(r))]

    exchange("gather", a_gather, [sized(afa.at[pl.ds(0, 3), :, pl.ds(0, 640)], pr_s.at[1], pr_r.at[1])])

    arrive("own")

    for d in range(2):
        arrive(("rq", d, 4))
    value = own_q(tok, z)[...].astype(F32) + oxq[...].astype(F32)
    for d in range(2):
        for j in range(2):
            value = value + rsq[d, 3, j].astype(F32)
    gfq[z] = value.astype(BF16)

    def q_gather_start():
        for dz in (4, 3, 5, 2, 6, 1, 7):
            remote(gfq.at[z], gfq.at[z], pr_s.at[2], pr_r.at[2], dev(0, 0, 0, dz)).start()

    q_whole = sized(gfq.at[pl.ds(0, 7)], pr_s.at[2], pr_r.at[2])
    send("q gather", q_gather_start, [q_whole], {"q gather": lambda count: q_whole})

    for cs in range(4):
        for d in range(2):
            arrive(("rc", d, 4, cs))
        value = own_c(tok, z, cs)[...].astype(F32) + oxc[:, pl.ds(*SETS[cs])].astype(F32)
        for d in range(2):
            for j in range(2):
                value = value + slot(d, 4, j, cs)[...].astype(F32)
        gfc[c_rows(z), pl.ds(*SETS[cs])] = value.astype(BF16)

    def ag_post(key, n, owner, cols, dz):
        ref = gfc.at[c_rows(owner), cols]
        post(key, [remote(ref, ref, ag_s.at[n], ag_r.at[n], dev(0, 0, 0, dz))])

    for cs in range(2):
        for d in range(2):
            ag_post(("second", d, cs), d * 2 + cs, z, pl.ds(*ENDS[cs]), 2 if d == 0 else 6)
    for d in range(2):
        ag_post(("next", d), 4 + d, z, pl.ds(0, 896), 1 if d == 0 else 7)

    arrive("e plane")
    eigen_sum = jnp.sum(jnp.sum(eb[...], axis=0))
    damping = 0.1 * eigen_sum / (FF * D)

    def invert(g, carry):
        inv[g] = 1.0 / (evb[g].astype(F32) + damping)
        return carry

    lax.fori_loop(0, GROUPS, invert, 0)

    for cs in range(2):
        for d in range(2):
            arrive(("second", d, cs))
            owner = z - 2 * sign(d)
            if cs == d:
                ag_post(("fourth", d), 6 + d, owner, pl.ds(*ENDS[cs]), 2 if d == 0 else 6)
            ag_post(("third", d, cs), 8 + d * 2 + cs, owner, pl.ds(*ENDS[cs]), 1 if d == 0 else 7)
    arrive("gather")
    post("core 2", [remote(afa.at[:, :, mine], afa.at[:, :, mine], co_s.at[1], co_r.at[1], dev(0, 0, 1, 0))])

    ids = jnp.zeros((1, 64), jnp.int32)
    lane = lax.broadcasted_iota(jnp.int32, (1, 64), 1)
    for s in range(64):
        ids = jnp.where(lane == s, qi[s], ids)
    doc = lax.broadcasted_iota(jnp.int32, (16, 256), 0)
    position = lax.broadcasted_iota(jnp.int32, (16, 256), 1)
    first = jnp.zeros((16, 256), jnp.int32)
    last = jnp.zeros((16, 256), jnp.int32)
    start = jnp.int32(0)
    for n in range(16):
        stop = start + dl[n]
        first = jnp.where(doc == n, start, first)
        last = jnp.where(doc == n, stop, last)
        start = stop
    member = ((position >= first) & (position < last)).astype(F32)

    arrive("q gather")
    arrive("core 2")

    def contract(g, carry):
        cols = pl.ds(pl.multiple_of(lax.rem(g, 2) * 128, 128), 128)
        half = lax.rem(g, 4) // 2
        rows = jnp.concatenate([gfq[2 * i + half, g // 4, :, cols].astype(F32) for i in range(4)], axis=0)
        turned = rows.T
        stacked = jnp.concatenate(
            [jnp.where(ids == q, turned, 0.0).astype(BF16) for q in range(Q)], axis=0
        )
        query_acts = jnp.concatenate([afa[i, 64:] for i in range(4)], axis=0)
        cand_acts = jnp.concatenate([afa[i, :64] for i in range(4)], axis=0)
        outer = jnp.dot(stacked, query_acts, preferred_element_type=F32)
        scale = inv[g]
        precond = jnp.concatenate(
            [(scale * outer[q * 128:(q + 1) * 128]).astype(BF16) for q in range(Q)], axis=0
        )
        mm[g] = lax.dot_general(
            cand_acts, precond, (((1,), (1,)), ((), ())), preferred_element_type=F32
        )
        return carry

    lax.fori_loop(0, GROUPS, contract, 0)
    for d in range(2):
        arrive(("next", d))
        arrive(("fourth", d))
        for cs in range(2):
            arrive(("third", d, cs))

    columns = []
    for q in range(Q):
        acc = jnp.zeros((256, 128), F32)
        for g in range(GROUPS):
            acc = acc + gfc[:, g * 128:(g + 1) * 128].astype(F32) * mm[g, :, q * 128:(q + 1) * 128]
        columns.append(acc)
    spread = jnp.dot(
        member, jnp.concatenate(columns, axis=1), precision=lax.Precision.HIGHEST, preferred_element_type=F32
    )
    column = lax.broadcasted_iota(jnp.int32, (16, 128), 1) - Q * lax.broadcasted_iota(jnp.int32, (16, 128), 0)
    scores = jnp.zeros((16, 128), F32)
    for q in range(Q):
        value = jnp.sum(spread[:, q * 128:(q + 1) * 128], axis=1, keepdims=True)
        scores = jnp.where(column == q, value, scores)
    fa[line] = jnp.sum(scores, axis=0, keepdims=True)
    early = dict(sends)
    sends.clear()
    all_to("f line", fa, line, 2, line_peer)
    late = dict(sends)
    sends.clear()
    sends.update(early)
    drain()
    sends.update(late)
    arrive("f line")
    fb[chip] = jnp.sum(fa[...], axis=0)
    all_to("f plane", fb, chip, 3, plane_peer)
    arrive("f plane")
    whole = jnp.broadcast_to(jnp.sum(fb[...], axis=0), (16, 128))
    place = lax.broadcasted_iota(jnp.int32, (16, Q), 1)
    result = jnp.zeros((16, Q), F32)
    for q in range(Q):
        value = jnp.sum(jnp.where(column == q, whole, 0.0), axis=1, keepdims=True)
        result = jnp.where(place == q, value, result)
    out[...] = result
    finish()


def local(*args):
    dma = pltpu.SemaphoreType.DMA
    vm = pltpu.VMEM
    return pl.pallas_call(
        kernel,
        out_shape=jax.ShapeDtypeStruct((16, Q), F32),
        in_specs=[pl.BlockSpec(memory_space=pl.ANY)] * 7 + [pl.BlockSpec(memory_space=pltpu.SMEM)] * 2,
        out_specs=pl.BlockSpec(memory_space=pltpu.VMEM),
        scratch_shapes=[
            vm((320, 1792), BF16), vm((320, 256), BF16), vm((GROUPS, 1792, 256), BF16), vm((256, 1024), BF16),
            vm((GROUPS, 128, 1024), BF16),
            vm((2, 256, 896), BF16), vm((2, 2, 64, 512), F32),
            vm((2, 4, 2, 32, 896), BF16), vm((2, 4, 2, 2, 16, 256), F32),
            vm((32, 896), BF16), vm((2, 16, 256), F32),
            vm((256, 896), BF16), vm((8, 2, 16, 256), BF16),
            vm((4, 80, 1024), F32), vm((4, 80, 512), F32), vm((16, 80, 128), F32), vm((4, 80, 1024), BF16),
            vm((GROUPS, 128, 1024), F32), vm((GROUPS, 256, 512), F32),
            vm((16, 1, 128), F32), vm((16, 1, 128), F32), vm((16, 1, 128), F32), vm((16, 1, 128), F32),
            dma((5 + GROUPS,)), dma((1,)),
            dma((2,)), dma((2, 4)),
            dma((2, 4)), dma((2, 4, 4)),
            dma((12,)), dma((12,)),
            dma((4,)), dma((4,)),
            dma((3,)), dma((3,)),
            dma((4,)), dma((4,)),
        ],
        name="influence",
        compiler_params=pltpu.CompilerParams(
            collective_id=0, has_side_effects=True, vmem_limit_bytes=63 << 20
        ),
    )(*args)


def solution(mesh):
    in_specs = (
        P(None, ("tok", "inp")),
        P(None, ("tok", "out")),
        P(None, ("tok", "inp")),
        P(None, ("tok", "out")),
        P(("tok", "inp"), "out"),
        P(("tok", "out"), "inp"),
        P("out", "inp"),
        P(),
        P(),
    )
    return jax.shard_map(local, mesh=mesh, in_specs=in_specs, out_specs=P(), check_vma=False)
```

```python
import jax
import jax.numpy as jnp
from jax import lax
from jax.experimental import pallas as pl
from jax.experimental.pallas import tpu as pltpu
from jax.sharding import PartitionSpec as P

D = 8192
FF = 28672
Q = 4
MESH = pl.DeviceIdType.MESH
F32 = jnp.float32
BF16 = jnp.bfloat16
GROUPS = 7
SETS = ((0, 256), (256, 256), (512, 256), (768, 128))
ENDS = ((0, 512), (512, 384))


def kernel(
    cg, ca, qg, qa, eo, ei, ev, dl, qi, out,
    xg, xa, eob, eib, evb, gpc, gpq, rsc, rsq, oxc, oxq, gfc, gfq,
    apk, rap, rda, afa, inv, mm, ea, eb, fa, fb,
    ld, evs, rq_s, rq_r, rc_s, rc_r, ag_s, ag_r, co_s, co_r, pr_s, pr_r, st_s, st_r,
):
    tok, o, z = lax.axis_index("tok"), lax.axis_index("out"), lax.axis_index("inp")
    x = tok * 2 + o // 8
    y = lax.rem(o // 2, 4)
    c = lax.rem(o, 2)
    chip = x * 4 + y
    line = c * 8 + z

    def dev(dx, dy, dc, dz):
        nx = lax.rem(x + dx, 4)
        ny = lax.rem(y + dy, 4)
        nc = lax.rem(c + dc, 2)
        return (nx // 2, lax.rem(nx, 2) * 8 + ny * 2 + nc, lax.rem(z + dz, 8))

    def remote(src, dst, ss, rs, where):
        return pltpu.make_async_remote_copy(
            src_ref=src, dst_ref=dst, send_sem=ss, recv_sem=rs, device_id=where, device_id_type=MESH
        )

    def line_peer(r):
        n = r - 1 + r // 15
        j = n // 2
        odd = lax.rem(j, 2)
        dz = 4 + odd * ((j + 1) // 2) + (1 - odd) * (8 - j // 2)
        return dev(0, 0, lax.rem(n, 2), dz)

    def plane_shift(r):
        n = r - 1 + r // 11
        return lax.rem(2 + n // 4, 4), lax.rem(2 + lax.rem(n, 4), 4)

    def plane_peer(r):
        dx, dy = plane_shift(r)
        return dev(dx, dy, 0, 0)

    def each(body):
        lax.fori_loop(1, 16, lambda r, carry: (body(r), carry)[1], 0)

    waits, sends = {}, {}

    def send(key, start, arrivals, departures):
        start()
        waits[key] = arrivals
        for name, leave in departures.items():
            sends.setdefault(name, []).append(leave)

    def arrive(key):
        for copy in waits.pop(key):
            copy.wait_recv()

    def drain():
        for leaves in sends.values():
            leaves[0](len(leaves)).wait_send()
        sends.clear()

    def finish():
        for key in list(waits):
            arrive(key)
        drain()

    def sized(ref, ss, rs):
        return remote(ref, ref, ss, rs, dev(0, 0, 1, 0))

    def post(key, copies):
        def start():
            for copy in copies:
                copy.start()
        send(key, start, copies, {(key, n): (lambda count, copy=copy: copy) for n, copy in enumerate(copies)})

    def exchange(key, copies, whole, unrolled=False):
        def start():
            if unrolled:
                for r in range(1, 16):
                    for copy in copies(r):
                        copy.start()
                return

            def body(r):
                for copy in copies(r):
                    copy.start()
            each(body)
        send(key, start, whole, {(key, n): (lambda count, copy=copy: copy) for n, copy in enumerate(whole)})

    loads = [
        pltpu.make_async_copy(ca, xa.at[pl.ds(0, 256)], ld.at[0]),
        pltpu.make_async_copy(qa, xa.at[pl.ds(256, 64)], ld.at[1]),
        pltpu.make_async_copy(ei, eib, ld.at[2]),
        pltpu.make_async_copy(cg, xg.at[pl.ds(0, 256)], ld.at[3]),
        pltpu.make_async_copy(qg, xg.at[pl.ds(256, 64)], ld.at[4]),
    ]

    def eo_load(g):
        return pltpu.make_async_copy(eo.at[:, pl.ds(pl.multiple_of(g * 256, 256), 256)], eob.at[g], ld.at[5 + g])

    def ev_load(g):
        row = pl.multiple_of((2 * g + tok) * 128, 128)
        return pltpu.make_async_copy(ev.at[pl.ds(row, 128)], evb.at[g], evs.at[0])

    for load in loads:
        load.start()
    for g in range(GROUPS):
        eo_load(g).start()

    barrier = pltpu.get_barrier_semaphore()

    def greet(r):
        pl.semaphore_signal(barrier, inc=1, device_id=line_peer(r), device_id_type=MESH)
        pl.semaphore_signal(barrier, inc=1, device_id=plane_peer(r), device_id_type=MESH)

    for r in range(1, 16):
        greet(r)
    for g in range(GROUPS):
        ev_load(g).start()

    for load in loads[:3]:
        load.wait()
    apart = jnp.dot(xa[...], eib[...], preferred_element_type=F32)
    for i in range(4):
        apk[i, :64] = apart[i * 64:(i + 1) * 64]
        apk[i, 64:] = apart[256 + i * 16:256 + (i + 1) * 16]

    for load in loads[3:]:
        load.wait()
    gpq[:, 1, :, 384:] = jnp.zeros((2, 64, 128), F32)

    def rotate(g):
        eo_load(g).wait()
        part = jnp.dot(xg[...], eob[g], preferred_element_type=F32)
        for t in range(2):
            gpc[t, :, g * 128:(g + 1) * 128] = part[:256, t * 128:(t + 1) * 128].astype(BF16)
            gpq[t, g // 4, :, (g % 4) * 128:(g % 4 + 1) * 128] = part[256:, t * 128:(t + 1) * 128]

    def c_rows(owner):
        return pl.ds(pl.multiple_of(lax.rem(owner + 16, 8) * 32, 32), 32)

    def q_rows(owner):
        return pl.ds(pl.multiple_of(lax.rem(owner + 16, 8) // 2 * 16, 16), 16)

    def q_cols(owner):
        return pl.ds(pl.multiple_of(lax.rem(owner + 16, 2) * 256, 256), 256)

    def own_q(t, owner):
        return gpq.at[t, :, q_rows(owner), q_cols(owner)]

    def own_c(t, owner, cs):
        return gpc.at[t, c_rows(owner), pl.ds(*SETS[cs])]

    def sign(d):
        return 1 if d == 0 else -1

    BOTH = slice(None)

    def rs_q(d, s):
        ss, rs = rq_s.at[d], rq_r.at[d, s - 1]
        dz = 1 if d == 0 else 7
        if s < 4:
            src = own_q(BOTH, z + sign(d) * (5 - s)) if s == d + 1 else rsq.at[d, s - 2]
            copies = [remote(src, rsq.at[d, s - 1], ss, rs, dev(0, 0, 0, dz))]
        else:
            copies = [remote(rsq.at[d, 2, t], rsq.at[d, 3, j], ss, rs, dev(2 * j, 0, 0, dz))
                      for j, t in ((1, 1 - tok), (0, tok))]

        def start():
            for copy in copies:
                copy.start()

        send(("rq", d, s), start, [sized(rsq.at[d, s - 1], ss, rs)],
             {("rq", d): lambda count: sized(rsq.at[d, pl.ds(0, count)], ss, rs)})

    def slot(d, s, t, cs):
        return rsc.at[d, s - 1, t, :, pl.ds(*SETS[cs])]

    def rs_c(d, s, cs):
        ss, rs = rc_s.at[d, cs], rc_r.at[d, s - 1, cs]
        dz = 1 if d == 0 else 7
        first = 1 if cs % 2 == d else 2
        if s < 4:
            src = own_c(BOTH, z + sign(d) * (5 - s), cs) if s == first else slot(d, s - 1, BOTH, cs)
            copies = [remote(src, slot(d, s, BOTH, cs), ss, rs, dev(0, 0, 0, dz))]
        else:
            copies = [remote(slot(d, 3, t, cs), slot(d, 4, j, cs), ss, rs, dev(2 * j, 0, 0, dz))
                      for j, t in ((1, 1 - tok), (0, tok))]

        def start():
            for copy in copies:
                copy.start()

        send(("rc", d, s, cs), start, [sized(slot(d, s, BOTH, cs), ss, rs)],
             {("rc", d, cs): lambda count: sized(rsc.at[d, pl.ds(0, count), :, :, pl.ds(*SETS[cs])], ss, rs)})

    def add_to(held, own):
        held[...] = (held[...].astype(F32) + own[...].astype(F32)).astype(held.dtype)

    def rs_step(s):
        for d in range(2 if s > 1 else 1):
            arrive(("rq", d, s))
            add_to(rsq.at[d, s - 1], own_q(BOTH, z + sign(d) * (4 - s)))
            rs_q(d, s + 1)
        for cs in range(4):
            for d in ((cs % 2, 1 - cs % 2) if s > 1 else (cs % 2,)):
                arrive(("rc", d, s, cs))
                add_to(slot(d, s, BOTH, cs), own_c(BOTH, z + sign(d) * (4 - s), cs))
                rs_c(d, s + 1, cs)

    for g in range(4):
        rotate(g)
    pl.semaphore_wait(barrier, 30)
    for cs in range(2):
        rs_c(cs, 1, cs)
    for cs in range(2):
        rs_c(1 - cs, 2, cs)
    other = pl.ds(pl.multiple_of((1 - c) * 512, 512), 512)
    mine = pl.ds(pl.multiple_of(c * 512, 512), 512)
    post("core 1", [remote(apk.at[:, :, other], rap, co_s.at[0], co_r.at[0], dev(0, 0, 1, 0))])
    for g in range(4, 7):
        rotate(g)
    rs_q(0, 1)
    rs_q(1, 2)
    for cs in range(2, 4):
        rs_c(cs - 2, 1, cs)
    for cs in range(2, 4):
        rs_c(3 - cs, 2, cs)
    post("own", [
        remote(own_q(1 - tok, z), oxq, co_s.at[2], co_r.at[2], dev(2, 0, 0, 0)),
        remote(gpc.at[1 - tok, c_rows(z)], oxc, co_s.at[3], co_r.at[3], dev(2, 0, 0, 0)),
    ])

    arrive("core 1")
    rap[...] = rap[...] + apk[:, :, mine]

    def a_scatter(r):
        dx, dy = plane_shift(r)
        cols = pl.ds(pl.multiple_of(lax.rem(y + dy, 4) * 128, 128), 128)
        return [remote(rap.at[lax.rem(x + dx, 4), :, cols], rda.at[chip], pr_s.at[0], pr_r.at[0], plane_peer(r))]

    exchange("scatter", a_scatter, [sized(rda.at[pl.ds(0, 15)], pr_s.at[0], pr_r.at[0])])
    rda[chip] = rap[x, :, pl.ds(pl.multiple_of(y * 128, 128), 128)]

    rs_step(1)

    total = jnp.zeros((8, 128), F32)
    pltpu.make_async_copy(evb, evb, evs.at[0]).wait()
    for g in range(GROUPS):
        for cb in range(8):
            vals = evb[g, :, cb * 128:(cb + 1) * 128].astype(F32)
            total = total + jnp.sum(vals.reshape(16, 8, 128), axis=0)

    def all_to(key, buf, place, kind, peer, unrolled=False):
        def body(r):
            return [remote(buf.at[place], buf.at[place], st_s.at[kind], st_r.at[kind], peer(r))]
        exchange(key, body, [sized(buf.at[pl.ds(0, 15)], st_s.at[kind], st_r.at[kind])], unrolled)

    ea[line] = jnp.sum(total, axis=0, keepdims=True)
    all_to("e line", ea, line, 0, line_peer)

    rs_step(2)

    arrive("e line")
    eb[chip] = jnp.sum(ea[...], axis=0)
    all_to("e plane", eb, chip, 1, plane_peer)

    rs_step(3)

    arrive("scatter")
    piece_cols = pl.ds(pl.multiple_of(c * 512 + y * 128, 128), 128)
    afa[x, :, piece_cols] = jnp.sum(rda[...], axis=0).astype(BF16)

    def a_gather(r):
        ref = afa.at[x, :, piece_cols]
        return [remote(ref, ref, pr_s.at[1], pr_r.at[1], plane_peer(r))]

    exchange("gather", a_gather, [sized(afa.at[pl.ds(0, 3), :, pl.ds(0, 640)], pr_s.at[1], pr_r.at[1])])

    arrive("own")

    for d in range(2):
        arrive(("rq", d, 4))
    value = own_q(tok, z)[...].astype(F32) + oxq[...].astype(F32)
    for d in range(2):
        for j in range(2):
            value = value + rsq[d, 3, j].astype(F32)
    gfq[z] = value.astype(BF16)

    def q_gather_start():
        for dz in (4, 3, 5, 2, 6, 1, 7):
            remote(gfq.at[z], gfq.at[z], pr_s.at[2], pr_r.at[2], dev(0, 0, 0, dz)).start()

    q_whole = sized(gfq.at[pl.ds(0, 7)], pr_s.at[2], pr_r.at[2])
    send("q gather", q_gather_start, [q_whole], {"q gather": lambda count: q_whole})

    def ag_post(key, n, owner, cols, dz):
        ref = gfc.at[c_rows(owner), cols]
        post(key, [remote(ref, ref, ag_s.at[n], ag_r.at[n], dev(0, 0, 0, dz))])

    for cs in range(4):
        for d in range(2):
            arrive(("rc", d, 4, cs))
        value = own_c(tok, z, cs)[...].astype(F32) + oxc[:, pl.ds(*SETS[cs])].astype(F32)
        for d in range(2):
            for j in range(2):
                value = value + slot(d, 4, j, cs)[...].astype(F32)
        gfc[c_rows(z), pl.ds(*SETS[cs])] = value.astype(BF16)
        if cs % 2 == 1:
            half = cs // 2
            for d in range(2):
                ag_post(("second", d, half), d * 2 + half, z, pl.ds(*ENDS[half]), 2 if d == 0 else 6)
    for d in range(2):
        ag_post(("next", d), 4 + d, z, pl.ds(0, 896), 1 if d == 0 else 7)

    arrive("e plane")
    eigen_sum = jnp.sum(jnp.sum(eb[...], axis=0))
    damping = 0.1 * eigen_sum / (FF * D)

    def invert(g, carry):
        inv[g] = 1.0 / (evb[g].astype(F32) + damping)
        return carry

    lax.fori_loop(0, GROUPS, invert, 0)

    for cs in range(2):
        for d in range(2):
            arrive(("second", d, cs))
            owner = z - 2 * sign(d)
            if cs == d:
                ag_post(("fourth", d), 6 + d, owner, pl.ds(*ENDS[cs]), 2 if d == 0 else 6)
            ag_post(("third", d, cs), 8 + d * 2 + cs, owner, pl.ds(*ENDS[cs]), 1 if d == 0 else 7)
    arrive("gather")
    post("core 2", [remote(afa.at[:, :, mine], afa.at[:, :, mine], co_s.at[1], co_r.at[1], dev(0, 0, 1, 0))])

    ids = jnp.zeros((1, 64), jnp.int32)
    lane = lax.broadcasted_iota(jnp.int32, (1, 64), 1)
    for s in range(64):
        ids = jnp.where(lane == s, qi[s], ids)
    lanes = lax.broadcasted_iota(jnp.int32, (1, 128), 1)
    first = jnp.zeros((1, 128), jnp.int32)
    last = jnp.zeros((1, 128), jnp.int32)
    start = jnp.int32(0)
    for n in range(16):
        stop = start + dl[n]
        for q in range(Q):
            first = jnp.where(lanes == q * 16 + n, start, first)
            last = jnp.where(lanes == q * 16 + n, stop, last)
        start = stop
    position = lax.broadcasted_iota(jnp.int32, (256, 128), 0)
    member = (position >= first) & (position < last)

    arrive("q gather")
    arrive("core 2")

    def contract(g, carry):
        cols = pl.ds(pl.multiple_of(lax.rem(g, 2) * 128, 128), 128)
        half = lax.rem(g, 4) // 2
        rows = jnp.concatenate([gfq[2 * i + half, g // 4, :, cols].astype(F32) for i in range(4)], axis=0)
        turned = rows.T
        stacked = jnp.concatenate(
            [jnp.where(ids == q, turned, 0.0).astype(BF16) for q in range(Q)], axis=0
        )
        query_acts = jnp.concatenate([afa[i, 64:] for i in range(4)], axis=0)
        cand_acts = jnp.concatenate([afa[i, :64] for i in range(4)], axis=0)
        outer = jnp.dot(stacked, query_acts, preferred_element_type=F32)
        scale = inv[g]
        precond = jnp.concatenate(
            [(scale * outer[q * 128:(q + 1) * 128]).astype(BF16) for q in range(Q)], axis=0
        )
        mm[g] = lax.dot_general(
            cand_acts, precond, (((1,), (1,)), ((), ())), preferred_element_type=F32
        )
        return carry

    lax.fori_loop(0, GROUPS, contract, 0)
    for d in range(2):
        arrive(("next", d))
        arrive(("fourth", d))
        for cs in range(2):
            arrive(("third", d, cs))

    by_query = jnp.zeros((256, 128), F32)
    for q in range(Q):
        acc = jnp.zeros((256, 128), F32)
        for g in range(GROUPS):
            acc = acc + gfc[:, g * 128:(g + 1) * 128].astype(F32) * mm[g, :, q * 128:(q + 1) * 128]
        token_scores = jnp.sum(acc, axis=1, keepdims=True)
        by_query = jnp.where((lanes >= q * 16) & (lanes < q * 16 + 16), token_scores, by_query)
    fa[line] = jnp.sum(jnp.where(member, by_query, 0.0), axis=0, keepdims=True)
    early = dict(sends)
    sends.clear()
    all_to("f line", fa, line, 2, line_peer, True)
    late = dict(sends)
    sends.clear()
    sends.update(early)
    drain()
    sends.update(late)
    arrive("f line")
    fb[chip] = jnp.sum(fa[...], axis=0)
    all_to("f plane", fb, chip, 3, plane_peer, True)
    arrive("f plane")
    scores = jnp.sum(fb[...], axis=0)
    for q in range(Q):
        out[q:q + 1, :] = scores[:, q * 16:(q + 1) * 16]
    finish()


def local(*args):
    dma = pltpu.SemaphoreType.DMA
    vm = pltpu.VMEM
    return pl.pallas_call(
        kernel,
        out_shape=jax.ShapeDtypeStruct((Q, 16), F32),
        in_specs=[pl.BlockSpec(memory_space=pl.ANY)] * 7 + [pl.BlockSpec(memory_space=pltpu.SMEM)] * 2,
        out_specs=pl.BlockSpec(memory_space=pltpu.VMEM),
        scratch_shapes=[
            vm((320, 1792), BF16), vm((320, 256), BF16), vm((GROUPS, 1792, 256), BF16), vm((256, 1024), BF16),
            vm((GROUPS, 128, 1024), BF16),
            vm((2, 256, 896), BF16), vm((2, 2, 64, 512), F32),
            vm((2, 4, 2, 32, 896), BF16), vm((2, 4, 2, 2, 16, 256), F32),
            vm((32, 896), BF16), vm((2, 16, 256), F32),
            vm((256, 896), BF16), vm((8, 2, 16, 256), BF16),
            vm((4, 80, 1024), F32), vm((4, 80, 512), F32), vm((16, 80, 128), F32), vm((4, 80, 1024), BF16),
            vm((GROUPS, 128, 1024), F32), vm((GROUPS, 256, 512), F32),
            vm((16, 1, 128), F32), vm((16, 1, 128), F32), vm((16, 1, 128), F32), vm((16, 1, 128), F32),
            dma((5 + GROUPS,)), dma((1,)),
            dma((2,)), dma((2, 4)),
            dma((2, 4)), dma((2, 4, 4)),
            dma((12,)), dma((12,)),
            dma((4,)), dma((4,)),
            dma((3,)), dma((3,)),
            dma((4,)), dma((4,)),
        ],
        name="influence",
        compiler_params=pltpu.CompilerParams(
            collective_id=0, has_side_effects=True, vmem_limit_bytes=63 << 20
        ),
    )(*args).T


def solution(mesh):
    in_specs = (
        P(None, ("tok", "inp")),
        P(None, ("tok", "out")),
        P(None, ("tok", "inp")),
        P(None, ("tok", "out")),
        P(("tok", "inp"), "out"),
        P(("tok", "out"), "inp"),
        P("out", "inp"),
        P(),
        P(),
    )
    return jax.shard_map(local, mesh=mesh, in_specs=in_specs, out_specs=P(), check_vma=False)
```

```python
import jax
import jax.numpy as jnp
from jax import lax
from jax.experimental import pallas as pl
from jax.experimental.pallas import tpu as pltpu
from jax.sharding import PartitionSpec as P

D = 8192
FF = 28672
Q = 4
MESH = pl.DeviceIdType.MESH
F32 = jnp.float32
BF16 = jnp.bfloat16
GROUPS = 7
SETS = ((0, 256), (256, 256), (512, 256), (768, 128))
ENDS = ((0, 512), (512, 384))


def kernel(
    cg, ca, qg, qa, eo, ei, ev, dl, qi, out,
    xg, xa, eob, eib, evb, gpc, gpq, rsc, rsq, oxc, oxq, gfc, gfq,
    apk, rap, rda, afa, inv, mm, ea, eb, fa, fb,
    ld, evs, rq_s, rq_r, rc_s, rc_r, ag_s, ag_r, co_s, co_r, pr_s, pr_r, st_s, st_r,
):
    tok, o, z = lax.axis_index("tok"), lax.axis_index("out"), lax.axis_index("inp")
    x = tok * 2 + o // 8
    y = lax.rem(o // 2, 4)
    c = lax.rem(o, 2)
    chip = x * 4 + y
    line = c * 8 + z

    def dev(dx, dy, dc, dz):
        nx = lax.rem(x + dx, 4)
        ny = lax.rem(y + dy, 4)
        nc = lax.rem(c + dc, 2)
        return (nx // 2, lax.rem(nx, 2) * 8 + ny * 2 + nc, lax.rem(z + dz, 8))

    def remote(src, dst, ss, rs, where):
        return pltpu.make_async_remote_copy(
            src_ref=src, dst_ref=dst, send_sem=ss, recv_sem=rs, device_id=where, device_id_type=MESH
        )

    def line_peer(r):
        n = r - 1 + r // 15
        j = n // 2
        odd = lax.rem(j, 2)
        dz = 4 + odd * ((j + 1) // 2) + (1 - odd) * (8 - j // 2)
        return dev(0, 0, lax.rem(n, 2), dz)

    def plane_shift(r):
        n = r - 1 + r // 11
        return lax.rem(2 + n // 4, 4), lax.rem(2 + lax.rem(n, 4), 4)

    def plane_peer(r):
        dx, dy = plane_shift(r)
        return dev(dx, dy, 0, 0)

    def each(body):
        lax.fori_loop(1, 16, lambda r, carry: (body(r), carry)[1], 0)

    waits, sends = {}, {}

    def send(key, start, arrivals, departures):
        start()
        waits[key] = arrivals
        for name, leave in departures.items():
            sends.setdefault(name, []).append(leave)

    def arrive(key):
        for copy in waits.pop(key):
            copy.wait_recv()

    def drain():
        for leaves in sends.values():
            leaves[0](len(leaves)).wait_send()
        sends.clear()

    def finish():
        for key in list(waits):
            arrive(key)
        drain()

    def sized(ref, ss, rs):
        return remote(ref, ref, ss, rs, dev(0, 0, 1, 0))

    def post(key, copies):
        def start():
            for copy in copies:
                copy.start()
        send(key, start, copies, {(key, n): (lambda count, copy=copy: copy) for n, copy in enumerate(copies)})

    def exchange(key, copies, whole, unrolled=False):
        def start():
            if unrolled:
                for r in range(1, 16):
                    for copy in copies(r):
                        copy.start()
                return

            def body(r):
                for copy in copies(r):
                    copy.start()
            each(body)
        send(key, start, whole, {(key, n): (lambda count, copy=copy: copy) for n, copy in enumerate(whole)})

    loads = [
        pltpu.make_async_copy(ca, xa.at[pl.ds(0, 256)], ld.at[0]),
        pltpu.make_async_copy(qa, xa.at[pl.ds(256, 64)], ld.at[1]),
        pltpu.make_async_copy(ei, eib, ld.at[2]),
        pltpu.make_async_copy(cg, xg.at[pl.ds(0, 256)], ld.at[3]),
        pltpu.make_async_copy(qg, xg.at[pl.ds(256, 64)], ld.at[4]),
    ]

    def eo_load(g):
        return pltpu.make_async_copy(eo.at[:, pl.ds(pl.multiple_of(g * 256, 256), 256)], eob.at[g], ld.at[5 + g])

    def ev_load(g):
        row = pl.multiple_of((2 * g + tok) * 128, 128)
        return pltpu.make_async_copy(ev.at[pl.ds(row, 128)], evb.at[g], evs.at[0])

    for load in loads:
        load.start()
    for g in range(GROUPS):
        eo_load(g).start()

    barrier = pltpu.get_barrier_semaphore()

    def greet(r):
        pl.semaphore_signal(barrier, inc=1, device_id=line_peer(r), device_id_type=MESH)
        pl.semaphore_signal(barrier, inc=1, device_id=plane_peer(r), device_id_type=MESH)

    for r in range(1, 16):
        greet(r)
    for g in range(GROUPS):
        ev_load(g).start()

    for load in loads[:3]:
        load.wait()
    apart = jnp.dot(xa[...], eib[...], preferred_element_type=F32)
    for i in range(4):
        apk[i, :64] = apart[i * 64:(i + 1) * 64]
        apk[i, 64:] = apart[256 + i * 16:256 + (i + 1) * 16]

    for load in loads[3:]:
        load.wait()
    gpq[:, 1, :, 384:] = jnp.zeros((2, 64, 128), F32)

    def rotate(g):
        eo_load(g).wait()
        part = jnp.dot(xg[...], eob[g], preferred_element_type=F32)
        for t in range(2):
            gpc[t, :, g * 128:(g + 1) * 128] = part[:256, t * 128:(t + 1) * 128].astype(BF16)
            gpq[t, g // 4, :, (g % 4) * 128:(g % 4 + 1) * 128] = part[256:, t * 128:(t + 1) * 128]

    def c_rows(owner):
        return pl.ds(pl.multiple_of(lax.rem(owner + 16, 8) * 32, 32), 32)

    def q_rows(owner):
        return pl.ds(pl.multiple_of(lax.rem(owner + 16, 8) // 2 * 16, 16), 16)

    def q_cols(owner):
        return pl.ds(pl.multiple_of(lax.rem(owner + 16, 2) * 256, 256), 256)

    def own_q(t, owner):
        return gpq.at[t, :, q_rows(owner), q_cols(owner)]

    def own_c(t, owner, cs):
        return gpc.at[t, c_rows(owner), pl.ds(*SETS[cs])]

    def sign(d):
        return 1 if d == 0 else -1

    BOTH = slice(None)

    def rs_q(d, s):
        ss, rs = rq_s.at[d], rq_r.at[d, s - 1]
        dz = 1 if d == 0 else 7
        if s < 4:
            src = own_q(BOTH, z + sign(d) * (5 - s)) if s == d + 1 else rsq.at[d, s - 2]
            copies = [remote(src, rsq.at[d, s - 1], ss, rs, dev(0, 0, 0, dz))]
        else:
            copies = [remote(rsq.at[d, 2, t], rsq.at[d, 3, j], ss, rs, dev(2 * j, 0, 0, dz))
                      for j, t in ((1, 1 - tok), (0, tok))]

        def start():
            for copy in copies:
                copy.start()

        send(("rq", d, s), start, [sized(rsq.at[d, s - 1], ss, rs)],
             {("rq", d): lambda count: sized(rsq.at[d, pl.ds(0, count)], ss, rs)})

    def slot(d, s, t, cs):
        return rsc.at[d, s - 1, t, :, pl.ds(*SETS[cs])]

    def rs_c(d, s, cs):
        ss, rs = rc_s.at[d, cs], rc_r.at[d, s - 1, cs]
        dz = 1 if d == 0 else 7
        first = 1 if cs % 2 == d else 2
        if s < 4:
            src = own_c(BOTH, z + sign(d) * (5 - s), cs) if s == first else slot(d, s - 1, BOTH, cs)
            copies = [remote(src, slot(d, s, BOTH, cs), ss, rs, dev(0, 0, 0, dz))]
        else:
            copies = [remote(slot(d, 3, t, cs), slot(d, 4, j, cs), ss, rs, dev(2 * j, 0, 0, dz))
                      for j, t in ((1, 1 - tok), (0, tok))]

        def start():
            for copy in copies:
                copy.start()

        send(("rc", d, s, cs), start, [sized(slot(d, s, BOTH, cs), ss, rs)],
             {("rc", d, cs): lambda count: sized(rsc.at[d, pl.ds(0, count), :, :, pl.ds(*SETS[cs])], ss, rs)})

    def add_to(held, own):
        held[...] = (held[...].astype(F32) + own[...].astype(F32)).astype(held.dtype)

    def rs_step(s):
        for d in range(2 if s > 1 else 1):
            arrive(("rq", d, s))
            add_to(rsq.at[d, s - 1], own_q(BOTH, z + sign(d) * (4 - s)))
            rs_q(d, s + 1)
        for cs in range(4):
            for d in ((cs % 2, 1 - cs % 2) if s > 1 else (cs % 2,)):
                arrive(("rc", d, s, cs))
                add_to(slot(d, s, BOTH, cs), own_c(BOTH, z + sign(d) * (4 - s), cs))
                rs_c(d, s + 1, cs)

    for g in range(4):
        rotate(g)
    pl.semaphore_wait(barrier, 30)
    other = pl.ds(pl.multiple_of((1 - c) * 512, 512), 512)
    mine = pl.ds(pl.multiple_of(c * 512, 512), 512)
    post("core 1", [remote(apk.at[:, :, other], rap, co_s.at[0], co_r.at[0], dev(0, 0, 1, 0))])
    for cs in range(2):
        rs_c(cs, 1, cs)
    for cs in range(2):
        rs_c(1 - cs, 2, cs)
    for g in range(4, 7):
        rotate(g)
    rs_q(0, 1)
    rs_q(1, 2)
    for cs in range(2, 4):
        rs_c(cs - 2, 1, cs)
    for cs in range(2, 4):
        rs_c(3 - cs, 2, cs)
    post("own", [
        remote(own_q(1 - tok, z), oxq, co_s.at[2], co_r.at[2], dev(2, 0, 0, 0)),
        remote(gpc.at[1 - tok, c_rows(z)], oxc, co_s.at[3], co_r.at[3], dev(2, 0, 0, 0)),
    ])

    arrive("core 1")
    rap[...] = rap[...] + apk[:, :, mine]

    def a_scatter(r):
        dx, dy = plane_shift(r)
        cols = pl.ds(pl.multiple_of(lax.rem(y + dy, 4) * 128, 128), 128)
        return [remote(rap.at[lax.rem(x + dx, 4), :, cols], rda.at[chip], pr_s.at[0], pr_r.at[0], plane_peer(r))]

    exchange("scatter", a_scatter, [sized(rda.at[pl.ds(0, 15)], pr_s.at[0], pr_r.at[0])])
    rda[chip] = rap[x, :, pl.ds(pl.multiple_of(y * 128, 128), 128)]

    rs_step(1)

    total = jnp.zeros((8, 128), F32)
    pltpu.make_async_copy(evb, evb, evs.at[0]).wait()
    for g in range(GROUPS):
        for cb in range(8):
            vals = evb[g, :, cb * 128:(cb + 1) * 128].astype(F32)
            total = total + jnp.sum(vals.reshape(16, 8, 128), axis=0)

    def all_to(key, buf, place, kind, peer, unrolled=False):
        def body(r):
            return [remote(buf.at[place], buf.at[place], st_s.at[kind], st_r.at[kind], peer(r))]
        exchange(key, body, [sized(buf.at[pl.ds(0, 15)], st_s.at[kind], st_r.at[kind])], unrolled)

    ea[line] = jnp.sum(total, axis=0, keepdims=True)
    all_to("e line", ea, line, 0, line_peer)

    rs_step(2)

    arrive("e line")
    eb[chip] = jnp.sum(ea[...], axis=0)
    all_to("e plane", eb, chip, 1, plane_peer)

    arrive("scatter")
    piece_cols = pl.ds(pl.multiple_of(c * 512 + y * 128, 128), 128)
    afa[x, :, piece_cols] = jnp.sum(rda[...], axis=0).astype(BF16)

    def a_gather(r):
        ref = afa.at[x, :, piece_cols]
        return [remote(ref, ref, pr_s.at[1], pr_r.at[1], plane_peer(r))]

    exchange("gather", a_gather, [sized(afa.at[pl.ds(0, 3), :, pl.ds(0, 640)], pr_s.at[1], pr_r.at[1])])

    rs_step(3)

    arrive("own")

    for d in range(2):
        arrive(("rq", d, 4))
    value = own_q(tok, z)[...].astype(F32) + oxq[...].astype(F32)
    for d in range(2):
        for j in range(2):
            value = value + rsq[d, 3, j].astype(F32)
    gfq[z] = value.astype(BF16)

    def q_gather_start():
        for dz in (4, 3, 5, 2, 6, 1, 7):
            remote(gfq.at[z], gfq.at[z], pr_s.at[2], pr_r.at[2], dev(0, 0, 0, dz)).start()

    q_whole = sized(gfq.at[pl.ds(0, 7)], pr_s.at[2], pr_r.at[2])
    send("q gather", q_gather_start, [q_whole], {"q gather": lambda count: q_whole})

    def ag_post(key, n, owner, cols, dz):
        ref = gfc.at[c_rows(owner), cols]
        post(key, [remote(ref, ref, ag_s.at[n], ag_r.at[n], dev(0, 0, 0, dz))])

    for cs in range(4):
        for d in range(2):
            arrive(("rc", d, 4, cs))
        value = own_c(tok, z, cs)[...].astype(F32) + oxc[:, pl.ds(*SETS[cs])].astype(F32)
        for d in range(2):
            for j in range(2):
                value = value + slot(d, 4, j, cs)[...].astype(F32)
        gfc[c_rows(z), pl.ds(*SETS[cs])] = value.astype(BF16)
        if cs % 2 == 1:
            half = cs // 2
            for d in range(2):
                ag_post(("second", d, half), d * 2 + half, z, pl.ds(*ENDS[half]), 2 if d == 0 else 6)
    for d in range(2):
        ag_post(("next", d), 4 + d, z, pl.ds(0, 896), 1 if d == 0 else 7)

    arrive("e plane")
    eigen_sum = jnp.sum(jnp.sum(eb[...], axis=0))
    damping = 0.1 * eigen_sum / (FF * D)

    def invert(g, carry):
        inv[g] = 1.0 / (evb[g].astype(F32) + damping)
        return carry

    lax.fori_loop(0, GROUPS, invert, 0)

    for cs in range(2):
        for d in range(2):
            arrive(("second", d, cs))
            owner = z - 2 * sign(d)
            if cs == d:
                ag_post(("fourth", d), 6 + d, owner, pl.ds(*ENDS[cs]), 2 if d == 0 else 6)
            ag_post(("third", d, cs), 8 + d * 2 + cs, owner, pl.ds(*ENDS[cs]), 1 if d == 0 else 7)
    arrive("gather")
    post("core 2", [remote(afa.at[:, :, mine], afa.at[:, :, mine], co_s.at[1], co_r.at[1], dev(0, 0, 1, 0))])

    ids = jnp.zeros((1, 64), jnp.int32)
    lane = lax.broadcasted_iota(jnp.int32, (1, 64), 1)
    for s in range(64):
        ids = jnp.where(lane == s, qi[s], ids)
    lanes = lax.broadcasted_iota(jnp.int32, (1, 128), 1)
    first = jnp.zeros((1, 128), jnp.int32)
    last = jnp.zeros((1, 128), jnp.int32)
    start = jnp.int32(0)
    for n in range(16):
        stop = start + dl[n]
        for q in range(Q):
            first = jnp.where(lanes == q * 16 + n, start, first)
            last = jnp.where(lanes == q * 16 + n, stop, last)
        start = stop
    position = lax.broadcasted_iota(jnp.int32, (256, 128), 0)
    member = (position >= first) & (position < last)

    arrive("q gather")
    arrive("core 2")

    def contract(g, carry):
        cols = pl.ds(pl.multiple_of(lax.rem(g, 2) * 128, 128), 128)
        half = lax.rem(g, 4) // 2
        rows = jnp.concatenate([gfq[2 * i + half, g // 4, :, cols].astype(F32) for i in range(4)], axis=0)
        turned = rows.T
        stacked = jnp.concatenate(
            [jnp.where(ids == q, turned, 0.0).astype(BF16) for q in range(Q)], axis=0
        )
        query_acts = jnp.concatenate([afa[i, 64:] for i in range(4)], axis=0)
        cand_acts = jnp.concatenate([afa[i, :64] for i in range(4)], axis=0)
        outer = jnp.dot(stacked, query_acts, preferred_element_type=F32)
        scale = inv[g]
        precond = jnp.concatenate(
            [(scale * outer[q * 128:(q + 1) * 128]).astype(BF16) for q in range(Q)], axis=0
        )
        mm[g] = lax.dot_general(
            cand_acts, precond, (((1,), (1,)), ((), ())), preferred_element_type=F32
        )
        return carry

    lax.fori_loop(0, GROUPS, contract, 0)
    for d in range(2):
        arrive(("next", d))
        arrive(("fourth", d))
        for cs in range(2):
            arrive(("third", d, cs))

    by_query = jnp.zeros((256, 128), F32)
    for q in range(Q):
        acc = jnp.zeros((256, 128), F32)
        for g in range(GROUPS):
            acc = acc + gfc[:, g * 128:(g + 1) * 128].astype(F32) * mm[g, :, q * 128:(q + 1) * 128]
        token_scores = jnp.sum(acc, axis=1, keepdims=True)
        by_query = jnp.where((lanes >= q * 16) & (lanes < q * 16 + 16), token_scores, by_query)
    fa[line] = jnp.sum(jnp.where(member, by_query, 0.0), axis=0, keepdims=True)
    early = dict(sends)
    sends.clear()
    all_to("f line", fa, line, 2, line_peer, True)
    late = dict(sends)
    sends.clear()
    sends.update(early)
    drain()
    sends.update(late)
    arrive("f line")
    fb[chip] = jnp.sum(fa[...], axis=0)
    all_to("f plane", fb, chip, 3, plane_peer, True)
    arrive("f plane")
    scores = jnp.sum(fb[...], axis=0)
    for q in range(Q):
        out[q:q + 1, :] = scores[:, q * 16:(q + 1) * 16]
    finish()


def local(*args):
    dma = pltpu.SemaphoreType.DMA
    vm = pltpu.VMEM
    return pl.pallas_call(
        kernel,
        out_shape=jax.ShapeDtypeStruct((Q, 16), F32),
        in_specs=[pl.BlockSpec(memory_space=pl.ANY)] * 7 + [pl.BlockSpec(memory_space=pltpu.SMEM)] * 2,
        out_specs=pl.BlockSpec(memory_space=pltpu.VMEM),
        scratch_shapes=[
            vm((320, 1792), BF16), vm((320, 256), BF16), vm((GROUPS, 1792, 256), BF16), vm((256, 1024), BF16),
            vm((GROUPS, 128, 1024), BF16),
            vm((2, 256, 896), BF16), vm((2, 2, 64, 512), F32),
            vm((2, 4, 2, 32, 896), BF16), vm((2, 4, 2, 2, 16, 256), F32),
            vm((32, 896), BF16), vm((2, 16, 256), F32),
            vm((256, 896), BF16), vm((8, 2, 16, 256), BF16),
            vm((4, 80, 1024), F32), vm((4, 80, 512), F32), vm((16, 80, 128), F32), vm((4, 80, 1024), BF16),
            vm((GROUPS, 128, 1024), F32), vm((GROUPS, 256, 512), F32),
            vm((16, 1, 128), F32), vm((16, 1, 128), F32), vm((16, 1, 128), F32), vm((16, 1, 128), F32),
            dma((5 + GROUPS,)), dma((1,)),
            dma((2,)), dma((2, 4)),
            dma((2, 4)), dma((2, 4, 4)),
            dma((12,)), dma((12,)),
            dma((4,)), dma((4,)),
            dma((3,)), dma((3,)),
            dma((4,)), dma((4,)),
        ],
        name="influence",
        compiler_params=pltpu.CompilerParams(
            collective_id=0, has_side_effects=True, vmem_limit_bytes=63 << 20
        ),
    )(*args).T


def solution(mesh):
    in_specs = (
        P(None, ("tok", "inp")),
        P(None, ("tok", "out")),
        P(None, ("tok", "inp")),
        P(None, ("tok", "out")),
        P(("tok", "inp"), "out"),
        P(("tok", "out"), "inp"),
        P("out", "inp"),
        P(),
        P(),
    )
    return jax.shard_map(local, mesh=mesh, in_specs=in_specs, out_specs=P(), check_vma=False)
```
